512 devices in a mesh: dp: 16 (over z, core), ctx: 8 (over y), mp: 4 (over x).
Axes of the slice: x: 4, y: 8, z: 8, core: 2. Of those that a mesh axis runs over, the one named last changes fastest.
Arguments:
- key_cache: bfloat16 [64, 2048, 1024], P('dp', 'ctx', 'mp'), may hold values from -5 to 5
- value_cache: bfloat16 [64, 2048, 1024], P('dp', 'ctx', 'mp'), may hold values from -5 to 5
- lengths: int32 [64], P('dp'), may hold values from 1 to 2048, as said below
- queries: bfloat16 [3, 64, 8192], P(None, 'dp', 'mp'), may hold values from -64 to 64
- fresh_pairs: bfloat16 [3, 2, 64, 1024], P(None, None, 'dp', 'mp'), may hold values from -5 to 5
- recent_inputs: bfloat16 [64, 3, 16384], P('dp', None, ('ctx', 'mp')), may hold values from -5 to 5
- scan_state: float32 [64, 16, 16384], P('dp', None, ('ctx', 'mp')), may hold values from -5 to 5
- mamba_inputs: bfloat16 [3, 2, 64, 16384], P(None, None, 'dp', ('ctx', 'mp')), may hold values from -5 to 5
- step_sizes: float32 [3, 64, 16384], P(None, 'dp', ('ctx', 'mp')), may hold values from 0.001 to 0.2
- filter_taps: bfloat16 [4, 16384], P(None, ('ctx', 'mp')), may hold values from -3 to 3
- filter_bias: float32 [16384], P(('ctx', 'mp')), may hold values from -3 to 3
- decay_logs: float32 [16, 16384], P(None, ('ctx', 'mp')), may hold values from 0 to 2.77
- skip_gain: float32 [16384], P(('ctx', 'mp')), may hold values from 0.5 to 1.5
- select_weight: bfloat16 [32, 16384], P(None, ('ctx', 'mp')), may hold values from -0.046875 to 0.046875
- target_group: int32 [64], P('dp'), may hold values from 0 to 15, as said below
- target_slot: int32 [64], P('dp'), may hold values from 0 to 3
Outputs:
- attended: bfloat16 [3, 64, 8192], P(None, 'dp', 'mp')
- mamba_output: bfloat16 [3, 64, 16384], P(None, 'dp', ('ctx', 'mp'))
The draws below stay inside these ranges and needn't reach their ends.
Inputs may be any that keep to these rules, and one draw needn't show every extreme that they name: The pairs (target_group, target_slot) name every slot of every group exactly once, and the 4 requests of one group go to 4 different groups. `lengths`: at least one request uses all 2048 positions.
All inputs are finite; a program needn't handle non-finite values.
Results may differ from the reference program's by a relative error of at most 0.0051.
Values may be sent and summed in bfloat16 or wider, within the bound.
A program may use at most 64 MiB of HBM per device.

```python
import math
import jax
import jax.numpy as jnp
from jax import lax

HEADS = 64
KV_HEADS = 8
HEAD = 128
INNER = 16384
STATE = 16
CONV = 4
STEPS = 3
SLOTS = 4
CTX_DEV = 256
REQUESTS = 64
CONTEXT = 2048
N_DP = 16
N_CTX = 8


def migration_plan(key):
    key = jax.random.fold_in(key, 101)
    keys = jax.random.split(key, 4)
    inner_order = jax.random.permutation(keys[0], N_DP)
    outer_order = jax.random.permutation(keys[1], N_DP)
    offsets = jax.random.permutation(keys[2], N_DP)[:SLOTS]
    rotation = jax.random.randint(keys[3], (N_DP,), 0, SLOTS)
    target_group = outer_order[(inner_order[:, None] + offsets[None, :]) % N_DP]
    target_slot = (jnp.arange(SLOTS)[None, :] + rotation[target_group]) % SLOTS
    return (target_group.reshape(-1).astype(jnp.int32), target_slot.reshape(-1).astype(jnp.int32))


def draw_target_group(key, part):
    target_group, target_slot = migration_plan(key)
    return target_group


def draw_target_slot(key, part):
    target_group, target_slot = migration_plan(key)
    return target_slot


def draw_lengths(key, part):
    key = jax.random.fold_in(key, 3)
    first_key, second_key = jax.random.split(key)
    drawn = jax.random.randint(first_key, (REQUESTS,), 1, CONTEXT + 1)
    longest = jax.random.randint(second_key, (), 0, REQUESTS)
    return jnp.where(jnp.arange(REQUESTS) == longest, CONTEXT, drawn).astype(jnp.int32)


def draw_queries(key, part):
    key = jax.random.fold_in(key, 5)
    entries = jnp.clip(jax.random.normal(key, (STEPS, REQUESTS, HEADS * HEAD)), -5.0, 5.0)
    return entries.astype(jnp.bfloat16)


def draw_fresh_pairs(key, part):
    key = jax.random.fold_in(key, 7)
    entries = jnp.clip(jax.random.normal(key, (STEPS, 2, REQUESTS, KV_HEADS * HEAD)), -5.0, 5.0)
    return entries.astype(jnp.bfloat16)


def draw_key_cache(key, part):
    key = jax.random.fold_in(key, 9)
    entries = jnp.clip(jax.random.normal(key, (REQUESTS, CONTEXT, KV_HEADS * HEAD)), -5.0, 5.0)
    return entries.astype(jnp.bfloat16)


def level_of(key, shape, cuts, smallest, top_value):
    def one(dim, blocks):
        heights = jax.random.uniform(jax.random.fold_in(jax.random.fold_in(key, 6), dim), (blocks,), jnp.float32, smallest / len(cuts), top_value / len(cuts))
        return jnp.repeat(jnp.exp(heights), shape[dim] // blocks).reshape((-1,) + (1,) * (len(shape) - dim - 1))

    loudness = one(*cuts[0])
    for cut in cuts[1:]:
        loudness = loudness * one(*cut)
    return loudness


def bell_draw(stream_key, extent, width, bound, cuts=(), held_as=jnp.bfloat16):
    values = width * jax.random.normal(stream_key, extent, jnp.float32)
    if cuts:
        values = values * level_of(stream_key, extent, cuts, -0.22, 0.18)
    return jnp.clip(values, -bound, bound).astype(held_as)


def setup_inputs(seed: int = 0) -> dict:
    arg_keys = jax.random.split(jax.random.key(seed), 17)
    return {
        "key_cache": draw_key_cache(jax.random.fold_in(arg_keys[16], 71), 0),
        "value_cache": bell_draw(arg_keys[1], (REQUESTS, CONTEXT, KV_HEADS * HEAD), 1.0, 5.0, ((0, 16), (1, 8), (2, 4))),
        "lengths": draw_lengths(jax.random.fold_in(arg_keys[16], 71), 0),
        "queries": draw_queries(jax.random.fold_in(arg_keys[16], 71), 0),
        "fresh_pairs": draw_fresh_pairs(jax.random.fold_in(arg_keys[16], 71), 0),
        "recent_inputs": bell_draw(arg_keys[5], (REQUESTS, CONV - 1, INNER), 1.0, 5.0, ((0, 16), (2, 32))),
        "scan_state": bell_draw(arg_keys[6], (REQUESTS, STATE, INNER), 1.0, 5.0, ((0, 16), (2, 32)), jnp.float32),
        "mamba_inputs": bell_draw(arg_keys[7], (STEPS, 2, REQUESTS, INNER), 1.0, 5.0, ((2, 16), (3, 32))),
        "step_sizes": jnp.clip(jnp.exp(math.log(0.2) - 5.2983173 * jax.random.uniform(arg_keys[8], (STEPS, REQUESTS, INNER), jnp.float32) ** level_of(arg_keys[8], (STEPS, REQUESTS, INNER), ((1, 16), (2, 32)), -0.2, 0.2)), 0.001, 0.2),
        "filter_taps": bell_draw(arg_keys[9], (CONV, INNER), CONV ** -0.5, 3.0, ((1, 32),)),
        "filter_bias": bell_draw(arg_keys[10], (INNER,), 0.5, 3.0, ((0, 32),), jnp.float32),
        "decay_logs": jnp.clip(2.77 * jax.random.uniform(arg_keys[11], (STATE, INNER), jnp.float32) ** level_of(arg_keys[11], (STATE, INNER), ((1, 32),), -0.2, 0.2), 0.0, 2.77),
        "skip_gain": jnp.clip(0.5 + 1.0 * jax.random.uniform(arg_keys[12], (INNER,), jnp.float32) ** level_of(arg_keys[12], (INNER,), ((0, 32),), -0.2, 0.2), 0.5, 1.5),
        "select_weight": bell_draw(arg_keys[13], (2 * STATE, INNER), INNER ** -0.5, 0.046875, ((1, 32),)),
        "target_group": draw_target_group(jax.random.fold_in(arg_keys[16], 71), 0),
        "target_slot": draw_target_slot(jax.random.fold_in(arg_keys[16], 71), 0),
    }


NEGATIVE = -1.0e30


def block_stats(question, key_rows, value_rows, usable):
    group_share = HEADS // KV_HEADS
    asked_rows = question.astype(jnp.float32).reshape(KV_HEADS, group_share, HEAD)
    keyed = key_rows.astype(jnp.float32).reshape(-1, KV_HEADS, HEAD)
    valued = value_rows.astype(jnp.float32).reshape(-1, KV_HEADS, HEAD)
    scores = jnp.einsum("gqd,pgd->gqp", asked_rows, keyed) * (HEAD ** -0.5)
    allowed = usable[None, None, :]
    scores = jnp.where(allowed, scores, NEGATIVE)
    highest = jnp.max(scores, axis=-1)
    weights = jnp.where(allowed, jnp.exp(scores - highest[..., None]), 0.0)
    weight_sum = jnp.sum(weights, axis=-1)
    rounded = lax.optimization_barrier(weights.astype(jnp.bfloat16))
    weighted = jnp.einsum("gqp,pgd->gqd", rounded.astype(jnp.float32), valued)
    return highest, weight_sum, weighted


def finish(question, highest, weight_sum, weighted, recent_keys, recent_values):
    group_share = HEADS // KV_HEADS
    asked_rows = question.astype(jnp.float32).reshape(KV_HEADS, group_share, HEAD)
    fresh_keys = recent_keys.astype(jnp.float32).reshape(-1, KV_HEADS, HEAD)
    fresh_values = recent_values.astype(jnp.float32).reshape(-1, KV_HEADS, HEAD)
    recent_scores = jnp.einsum("gqd,ngd->gqn", asked_rows, fresh_keys) * (HEAD ** -0.5)
    overall = jnp.maximum(highest, jnp.max(recent_scores, axis=-1))
    retain = jnp.exp(highest - overall)
    recent_weights = jnp.exp(recent_scores - overall[..., None])
    numerator = weighted * retain[..., None] + jnp.einsum("gqn,ngd->gqd", recent_weights, fresh_values, precision=lax.Precision.HIGHEST)
    denominator = weight_sum * retain + jnp.sum(recent_weights, axis=-1)
    return (numerator / denominator[..., None]).reshape(HEADS * HEAD).astype(jnp.bfloat16)


def attend(question, key_rows, value_rows, length, recent_keys, recent_values):
    positions = jnp.arange(CONTEXT, dtype=jnp.int32).reshape(N_CTX, CTX_DEV)

    def one_block(keys_block, values_block, places):
        return block_stats(question, keys_block, values_block, places < length)

    highest, weight_sum, weighted = jax.vmap(one_block)(key_rows.reshape(N_CTX, CTX_DEV, -1), value_rows.reshape(N_CTX, CTX_DEV, -1), positions)
    overall_block = jnp.max(highest, axis=0)
    factor = jnp.exp(highest - overall_block)
    summed = jnp.sum(weight_sum * factor, axis=0)
    combined = jnp.sum(weighted * factor[..., None], axis=0)
    return finish(question, overall_block, summed, combined, recent_keys, recent_values)


def mamba_step(recent_rows, hidden_state, fresh_input, gate_input, step_rows, filter_taps, filter_bias, decay_logs, skip_gain, select_weight):
    window = jnp.concatenate([recent_rows, fresh_input[:, None, :]], axis=1)
    filtered = jnp.sum(window.astype(jnp.float32) * filter_taps.astype(jnp.float32)[None], axis=1) + filter_bias
    filtered = lax.optimization_barrier((filtered * jax.nn.sigmoid(filtered)).astype(jnp.bfloat16))
    as_float = filtered.astype(jnp.float32)
    selection = jnp.einsum("ri,si->rs", as_float, select_weight.astype(jnp.float32))
    input_select = selection[:, :STATE]
    output_select = selection[:, STATE:]
    decays = jnp.exp(-step_rows[:, None, :] * jnp.exp(decay_logs)[None])
    new_state = decays * hidden_state + step_rows[:, None, :] * input_select[:, :, None] * as_float[:, None, :]
    readout = jnp.sum(output_select[:, :, None] * new_state, axis=1) + skip_gain * as_float
    result = (readout * jax.nn.silu(gate_input.astype(jnp.float32))).astype(jnp.bfloat16)
    return window[:, 1:], new_state, result


def reference(key_cache, value_cache, lengths, queries, fresh_pairs, recent_inputs, scan_state, mamba_inputs, step_sizes, filter_taps, filter_bias, decay_logs, skip_gain, select_weight, target_group, target_slot):
    landing = (target_group * SLOTS + target_slot).astype(jnp.int32)
    anchor = jnp.zeros((REQUESTS,), jnp.int32).at[landing].set(jnp.arange(REQUESTS, dtype=jnp.int32))

    def opening(request):
        return attend(queries[0, request], key_cache[request], value_cache[request], lengths[request], fresh_pairs[0, 0, request][None], fresh_pairs[0, 1, request][None])

    attended = [lax.map(opening, jnp.arange(REQUESTS, dtype=jnp.int32))]
    for number in (1, 2):
        def later(row_index, number=number):
            request = anchor[row_index]
            key_list = [fresh_pairs[0, 0, request]] + [fresh_pairs[later_step, 0, row_index] for later_step in range(1, number + 1)]
            value_list = [fresh_pairs[0, 1, request]] + [fresh_pairs[later_step, 1, row_index] for later_step in range(1, number + 1)]
            return attend(queries[number, row_index], key_cache[request], value_cache[request], lengths[request], jnp.stack(key_list), jnp.stack(value_list))

        attended.append(lax.map(later, jnp.arange(REQUESTS, dtype=jnp.int32)))
    carried, hidden_state, result = mamba_step(recent_inputs, scan_state, mamba_inputs[0, 0], mamba_inputs[0, 1], step_sizes[0], filter_taps, filter_bias, decay_logs, skip_gain, select_weight)
    mixed_out = [result]
    carried = carried[anchor]
    hidden_state = hidden_state[anchor]
    for number in (1, 2):
        carried, hidden_state, result = mamba_step(carried, hidden_state, mamba_inputs[number, 0], mamba_inputs[number, 1], step_sizes[number], filter_taps, filter_bias, decay_logs, skip_gain, select_weight)
        mixed_out.append(result)
    return jnp.stack(attended), jnp.stack(mixed_out)
```

```python
import functools

import jax
import jax.numpy as jnp
from jax import lax
from jax.experimental import pallas as pl
from jax.experimental.pallas import tpu as pltpu
from jax.sharding import PartitionSpec as P

HEAD = 128
NEGATIVE = -1e30
SCALE = HEAD**-0.5
MESH = pl.DeviceIdType.MESH
F32 = jnp.float32
BF16 = jnp.bfloat16

N_DP = 16
N_CTX = 8
N_MP = 4
SLOTS = 4
BLOCK = 256
CHAN = 512
CHUNKS = CHAN // 128
STATE = 16

ROW_Q = 0
ROW_F = 32
ROW_M = 40
ROW_S = 56
MSG = 64


def kernel(
    lengths,
    target_group,
    target_slot,
    key_ref,
    value_ref,
    query_ref,
    fresh_ref,
    recent_ref,
    state_ref,
    inputs_ref,
    steps_ref,
    taps_ref,
    bias_ref,
    decay_ref,
    skip_ref,
    select_ref,
    att_ref,
    mam_ref,
    table_out,
    table_in,
    member,
    rows_new,
    rows_old,
    ask_out,
    ask_in,
    moved,
    asked,
    fresh_rows,
    filt,
    sel_out,
    sel_mp,
    sel_sum,
    sel_ctx,
    part_out,
    part_in,
    fin_out,
    fin_in,
    scan_rows,
    mam_rows,
    mam_out,
    mam_in,
    ans_out,
    ans_in,
    back_rows,
    send_sem,
    recv_sem,
):
    d = lax.axis_index("dp")
    c = lax.axis_index("ctx")
    m = lax.axis_index("mp")

    def over_dp(fn):
        def body(k, carry):
            fn(lax.rem(d + k, N_DP))
            return carry

        lax.fori_loop(1, N_DP, body, 0)

    def over_ctx(fn):
        def body(k, carry):
            fn(lax.rem(c + k, N_CTX))
            return carry

        lax.fori_loop(1, N_CTX, body, 0)

    def over_mp(fn):
        def body(k, carry):
            fn(lax.rem(m + k, N_MP))
            return carry

        lax.fori_loop(1, N_MP, body, 0)

    def send(src, dst, phase, device):
        pltpu.make_async_remote_copy(
            src_ref=src,
            dst_ref=dst,
            send_sem=send_sem.at[phase],
            recv_sem=recv_sem.at[phase],
            device_id=device,
            device_id_type=MESH,
        ).start()

    def arrived(buffer, phase, count):
        part = buffer.at[pl.ds(0, count)]
        pltpu.make_async_copy(part, part, recv_sem.at[phase]).wait()

    def sent(buffer, phase, count):
        part = buffer.at[pl.ds(0, count)]
        pltpu.make_async_copy(part, part, send_sem.at[phase]).wait()

    barrier = pltpu.get_barrier_semaphore()
    over_dp(lambda p: pl.semaphore_signal(barrier, inc=1, device_id={"dp": p}, device_id_type=MESH))
    over_ctx(lambda p: pl.semaphore_signal(barrier, inc=1, device_id={"ctx": p}, device_id_type=MESH))
    over_mp(lambda p: pl.semaphore_signal(barrier, inc=1, device_id={"mp": p}, device_id_type=MESH))

    lane = lax.broadcasted_iota(jnp.int32, (1, 128), 1)
    landing = jnp.full((1, 128), -1, jnp.int32)
    for s in range(SLOTS):
        landing = jnp.where(lane == s, target_group[s] * SLOTS + target_slot[s], landing)
    table_out[0] = landing
    table_in[d] = landing
    pl.semaphore_wait(barrier, (N_DP - 1) + (N_CTX - 1) + (N_MP - 1))

    over_dp(lambda p: send(table_out.at[0], table_in.at[d], 0, {"dp": p}))

    for t in (1, 2):
        q = query_ref[t].astype(F32)
        for j in range(16):
            rows_new[pl.ds(ROW_Q + (t - 1) * 16 + j, SLOTS, stride=MSG), :] = q[:, j * 128 : (j + 1) * 128]
        for kv in range(2):
            f = fresh_ref[t, kv].astype(F32)
            for h in range(2):
                rows_new[pl.ds(ROW_F + (t - 1) * 4 + kv * 2 + h, SLOTS, stride=MSG), :] = f[:, h * 128 : (h + 1) * 128]
        for w in range(2):
            x = inputs_ref[t, w].astype(F32)
            for ch in range(CHUNKS):
                rows_new[pl.ds(ROW_M + (t - 1) * 8 + w * 4 + ch, SLOTS, stride=MSG), :] = x[:, ch * 128 : (ch + 1) * 128]
        x = steps_ref[t]
        for ch in range(CHUNKS):
            rows_new[pl.ds(ROW_S + (t - 1) * 4 + ch, SLOTS, stride=MSG), :] = x[:, ch * 128 : (ch + 1) * 128]
    q = query_ref[0].astype(F32)
    for j in range(16):
        rows_old[pl.ds(j, SLOTS, stride=24), :] = q[:, j * 128 : (j + 1) * 128]
    for kv in range(2):
        f = fresh_ref[0, kv].astype(F32)
        for h in range(2):
            rows_old[pl.ds(16 + kv * 2 + h, SLOTS, stride=24), :] = f[:, h * 128 : (h + 1) * 128]

    arrived(table_in, 0, N_DP - 1)
    table = table_in[...].reshape(N_DP, 128)
    for i in range(SLOTS):
        hit = jnp.where(table == d * SLOTS + i, 1.0, 0.0).astype(F32)
        member[i] = jnp.broadcast_to(jnp.max(hit, axis=1, keepdims=True), (N_DP, 128))

    def ask(p):
        total = rows_new[0:MSG, :] * member[0, pl.ds(p, 1), :]
        for i in range(1, SLOTS):
            total += rows_new[i * MSG : (i + 1) * MSG, :] * member[i, pl.ds(p, 1), :]
        return total.astype(BF16)

    def ask_one(p):
        ask_out[p] = ask(p)
        send(ask_out.at[p], ask_in.at[d], 1, {"dp": p})

    over_dp(ask_one)
    ask_in[d] = ask(d)

    taps = taps_ref[...].astype(F32)
    bias = bias_ref[...]
    recent = recent_ref[...].astype(F32)
    window = [recent[:, k, :] for k in range(3)] + [inputs_ref[0, 0].astype(F32)]

    def filtered(parts):
        total = parts[0] * taps[0:1, :]
        for k in range(1, 4):
            total += parts[k] * taps[k : k + 1, :]
        total += bias
        return (total * jax.nn.sigmoid(total)).astype(BF16).astype(F32)

    filt[0, 0:SLOTS, :] = filtered(window)
    rates = jnp.exp(decay_ref[...])

    arrived(ask_in, 1, N_DP - 1)
    for s in range(SLOTS):
        moved[s * MSG : (s + 1) * MSG, :] = ask_in[target_group[s]].astype(F32)

    def moved_rows(row):
        return jnp.concatenate([moved[pl.ds(row + ch, SLOTS, stride=MSG), :] for ch in range(CHUNKS)], axis=1)

    for t in (1, 2):
        window = window[1:] + [moved_rows(ROW_M + (t - 1) * 8)]
        filt[t, 0:SLOTS, :] = filtered(window)
    weight = select_ref[...]
    weight = jnp.concatenate([weight] * SLOTS, axis=0)
    own = lax.broadcasted_iota(jnp.int32, (8, 128), 1) // 32 == lax.broadcasted_iota(jnp.int32, (8, 128), 0)
    picks = []
    for t in range(3):
        product = lax.dot_general(
            filt[t].astype(BF16), weight, (((1,), (1,)), ((), ())), preferred_element_type=F32
        )
        picks.append(jnp.sum(jnp.where(own, product, 0.0), axis=0, keepdims=True))
    sel_out[0] = jnp.concatenate(picks + [jnp.zeros((5, 128), F32)], axis=0)
    sel_mp[m] = sel_out[0]
    over_mp(lambda p: send(sel_out.at[0], sel_mp.at[m], 2, {"mp": p}))

    positions = lax.broadcasted_iota(jnp.int32, (1, BLOCK), 1) + c * BLOCK
    lanes = lax.broadcasted_iota(jnp.int32, (24, 128), 1)
    for s in range(SLOTS):
        usable = positions < lengths[s]
        for h in range(2):
            unit = s * 2 + h
            asks = jnp.concatenate(
                [rows_old[s * 24 + h * 8 : s * 24 + h * 8 + 8, :]]
                + [moved[s * MSG + ROW_Q + t * 16 + h * 8 : s * MSG + ROW_Q + t * 16 + h * 8 + 8, :] for t in range(2)],
                axis=0,
            )
            asked[unit] = asks
            fresh_rows[unit] = jnp.concatenate(
                [rows_old[s * 24 + 16 + h : s * 24 + 17 + h, :]]
                + [moved[s * MSG + ROW_F + t * 4 + h : s * MSG + ROW_F + t * 4 + h + 1, :] for t in range(2)]
                + [rows_old[s * 24 + 18 + h : s * 24 + 19 + h, :]]
                + [moved[s * MSG + ROW_F + t * 4 + 2 + h : s * MSG + ROW_F + t * 4 + 3 + h, :] for t in range(2)]
                + [jnp.zeros((2, 128), F32)],
                axis=0,
            )
            keys = key_ref[s, :, h * 128 : (h + 1) * 128]
            values = value_ref[s, :, h * 128 : (h + 1) * 128]
            scores = (
                lax.dot_general(asks.astype(BF16), keys, (((1,), (1,)), ((), ())), preferred_element_type=F32) * SCALE
            )
            scores = jnp.where(usable, scores, NEGATIVE)
            top = jnp.max(scores, axis=1, keepdims=True).astype(BF16).astype(F32)
            weights = jnp.where(usable, jnp.exp(scores - top), 0.0)
            total = jnp.sum(weights, axis=1, keepdims=True)
            mixed = jnp.dot(weights.astype(BF16), values, preferred_element_type=F32)
            high = total.astype(BF16).astype(F32)
            stats = jnp.where(lanes == 0, top, jnp.where(lanes == 1, high, total - high))
            part_out[unit] = jnp.concatenate([mixed, stats], axis=0).astype(BF16)
    part_in[c] = part_out[c]
    over_ctx(lambda p: send(part_out.at[p], part_in.at[c], 3, {"ctx": p}))

    arrived(sel_mp, 2, N_MP - 1)
    total = sel_mp[0]
    for k in range(1, N_MP):
        total += sel_mp[k]
    sel_sum[0] = total
    sel_ctx[c] = total
    over_ctx(lambda p: send(sel_sum.at[0], sel_ctx.at[c], 4, {"ctx": p}))

    arrived(part_in, 3, N_CTX - 1)
    asks = asked[c]
    fresh = fresh_rows[c]
    step_of = lax.broadcasted_iota(jnp.int32, (24, 1), 0) // 8
    parts = [part_in[k].astype(F32) for k in range(N_CTX)]
    tops = [part[24:48, 0:1] for part in parts]
    overall = tops[0]
    for k in range(1, N_CTX):
        overall = jnp.maximum(overall, tops[k])
    recents = []
    for u in range(3):
        score = jnp.sum(asks * fresh[u : u + 1, :], axis=1, keepdims=True) * SCALE
        score = jnp.where(step_of >= u, score, NEGATIVE)
        recents.append(score)
        overall = jnp.maximum(overall, score)
    numerator = jnp.zeros((24, 128), F32)
    denominator = jnp.zeros((24, 1), F32)
    for k in range(N_CTX):
        keep = jnp.exp(tops[k] - overall)
        numerator += parts[k][0:24, :] * keep
        denominator += (parts[k][24:48, 1:2] + parts[k][24:48, 2:3]) * keep
    for u in range(3):
        keep = jnp.where(step_of >= u, jnp.exp(recents[u] - overall), 0.0)
        numerator += fresh[3 + u : 4 + u, :] * keep
        denominator += keep
    done = jnp.concatenate([numerator / denominator, jnp.zeros((8, 128), F32)], axis=0).astype(BF16)
    fin_out[0] = done
    fin_in[c] = done
    over_ctx(lambda p: send(fin_out.at[0], fin_in.at[c], 5, {"ctx": p}))

    arrived(sel_ctx, 4, N_CTX - 1)
    total = sel_ctx[0]
    for k in range(1, N_CTX):
        total += sel_ctx[k]
    columns = jnp.transpose(total)
    sizes = [steps_ref[0]] + [moved_rows(ROW_S + (t - 1) * 4) for t in (1, 2)]
    gates = [inputs_ref[0, 1].astype(F32)] + [moved_rows(ROW_M + (t - 1) * 8 + 4) for t in (1, 2)]
    inputs = [filt[t, 0:SLOTS, :] for t in range(3)]
    for s in range(SLOTS):
        hidden = state_ref[s]
        for t in range(3):
            size = sizes[t][s : s + 1, :]
            into = columns[s * 32 : s * 32 + 16, t : t + 1]
            out = columns[s * 32 + 16 : s * 32 + 32, t : t + 1]
            hidden = jnp.exp(-size * rates) * hidden + into * (size * inputs[t][s : s + 1, :])
            scan_rows[t, s : s + 1, :] = jnp.sum(out * hidden, axis=0, keepdims=True)
    for t in range(3):
        result = (scan_rows[t, 0:SLOTS, :] + skip_ref[...] * inputs[t]) * (gates[t] * jax.nn.sigmoid(gates[t]))
        if t == 0:
            mam_ref[0] = result.astype(BF16)
        else:
            for ch in range(CHUNKS):
                mam_rows[pl.ds((t - 1) * 4 + ch, SLOTS, stride=8), :] = result[:, ch * 128 : (ch + 1) * 128]

    def leaves(s, p):
        return jnp.where(target_group[s] == p, 1.0, 0.0).astype(F32)

    def mam_message(p):
        total = mam_rows[0:8, :] * leaves(0, p)
        for s in range(1, SLOTS):
            total += mam_rows[s * 8 : (s + 1) * 8, :] * leaves(s, p)
        return total

    def mam_one(p):
        mam_out[p] = mam_message(p)
        send(mam_out.at[p], mam_in.at[d], 6, {"dp": p})

    over_dp(mam_one)
    mam_in[d] = mam_message(d)

    arrived(fin_in, 5, N_CTX - 1)
    finished = [fin_in[k].astype(F32) for k in range(N_CTX)]
    for s in range(SLOTS):
        for h in range(2):
            back_rows[s * 32 + h * 16 : s * 32 + h * 16 + 16, :] = finished[s * 2 + h][8:24, :]

    def ans_message(p):
        total = back_rows[0:32, :] * leaves(0, p)
        for s in range(1, SLOTS):
            total += back_rows[s * 32 : (s + 1) * 32, :] * leaves(s, p)
        return total.astype(BF16)

    def ans_one(p):
        ans_out[p] = ans_message(p)
        send(ans_out.at[p], ans_in.at[d], 7, {"dp": p})

    over_dp(ans_one)
    ans_in[d] = ans_message(d)
    for s in range(SLOTS):
        for h in range(2):
            rows_old[s * 24 + h * 8 : s * 24 + h * 8 + 8, :] = finished[s * 2 + h][0:8, :]
    for j in range(16):
        att_ref[0, :, j * 128 : (j + 1) * 128] = rows_old[pl.ds(j, SLOTS, stride=24), :].astype(BF16)

    arrived(mam_in, 6, N_DP - 1)
    for i in range(SLOTS):
        total = mam_in[0] * member[i, 0:1, :]
        for g in range(1, N_DP):
            total += mam_in[g] * member[i, g : g + 1, :]
        mam_rows[i * 8 : (i + 1) * 8, :] = total
    for t in (1, 2):
        for ch in range(CHUNKS):
            mam_ref[t, :, ch * 128 : (ch + 1) * 128] = mam_rows[
                pl.ds((t - 1) * 4 + ch, SLOTS, stride=8), :
            ].astype(BF16)
    arrived(ans_in, 7, N_DP - 1)
    for i in range(SLOTS):
        total = ans_in[0].astype(F32) * member[i, 0:1, :]
        for g in range(1, N_DP):
            total += ans_in[g].astype(F32) * member[i, g : g + 1, :]
        back_rows[i * 32 : (i + 1) * 32, :] = total
    for t in (1, 2):
        for h in range(2):
            for j in range(8):
                att_ref[t, :, (h * 8 + j) * 128 : (h * 8 + j + 1) * 128] = back_rows[
                    pl.ds(h * 16 + (t - 1) * 8 + j, SLOTS, stride=32), :
                ].astype(BF16)

    sent(table_in, 0, N_DP - 1)
    sent(ask_out, 1, N_DP - 1)
    sent(sel_mp, 2, N_MP - 1)
    sent(part_out, 3, N_CTX - 1)
    sent(sel_ctx, 4, N_CTX - 1)
    sent(fin_in, 5, N_CTX - 1)
    sent(mam_out, 6, N_DP - 1)
    sent(ans_out, 7, N_DP - 1)


def on_device(
    key_cache,
    value_cache,
    lengths,
    queries,
    fresh_pairs,
    recent_inputs,
    scan_state,
    mamba_inputs,
    step_sizes,
    filter_taps,
    filter_bias,
    decay_logs,
    skip_gain,
    select_weight,
    target_group,
    target_slot,
):
    smem = pl.BlockSpec(memory_space=pltpu.SMEM)
    vmem = pl.BlockSpec(memory_space=pltpu.VMEM)
    return pl.pallas_call(
        kernel,
        out_shape=(
            jax.ShapeDtypeStruct((3, SLOTS, 2048), BF16),
            jax.ShapeDtypeStruct((3, SLOTS, CHAN), BF16),
        ),
        in_specs=[smem] * 3 + [vmem] * 13,
        out_specs=(vmem, vmem),
        scratch_shapes=[
            pltpu.VMEM((1, 1, 128), jnp.int32),
            pltpu.VMEM((N_DP, 1, 128), jnp.int32),
            pltpu.VMEM((SLOTS, N_DP, 128), F32),
            pltpu.VMEM((SLOTS * MSG, 128), F32),
            pltpu.VMEM((SLOTS * 24, 128), F32),
            pltpu.VMEM((N_DP, MSG, 128), BF16),
            pltpu.VMEM((N_DP, MSG, 128), BF16),
            pltpu.VMEM((SLOTS * MSG, 128), F32),
            pltpu.VMEM((8, 24, 128), F32),
            pltpu.VMEM((8, 8, 128), F32),
            pltpu.VMEM((3, 8, CHAN), F32),
            pltpu.VMEM((1, 8, 128), F32),
            pltpu.VMEM((N_MP, 8, 128), F32),
            pltpu.VMEM((1, 8, 128), F32),
            pltpu.VMEM((N_CTX, 8, 128), F32),
            pltpu.VMEM((N_CTX, 48, 128), BF16),
            pltpu.VMEM((N_CTX, 48, 128), BF16),
            pltpu.VMEM((1, 32, 128), BF16),
            pltpu.VMEM((N_CTX, 32, 128), BF16),
            pltpu.VMEM((3, 8, CHAN), F32),
            pltpu.VMEM((SLOTS * 8, 128), F32),
            pltpu.VMEM((N_DP, 8, 128), F32),
            pltpu.VMEM((N_DP, 8, 128), F32),
            pltpu.VMEM((N_DP, 32, 128), BF16),
            pltpu.VMEM((N_DP, 32, 128), BF16),
            pltpu.VMEM((SLOTS * 32, 128), F32),
            pltpu.SemaphoreType.DMA((8,)),
            pltpu.SemaphoreType.DMA((8,)),
        ],
        compiler_params=pltpu.CompilerParams(
            collective_id=0, has_side_effects=True, vmem_limit_bytes=32 * 2**20
        ),
    )(
        lengths,
        target_group,
        target_slot,
        key_cache,
        value_cache,
        queries,
        fresh_pairs,
        recent_inputs,
        scan_state,
        mamba_inputs,
        step_sizes,
        filter_taps,
        filter_bias.reshape(1, CHAN),
        decay_logs,
        skip_gain.reshape(1, CHAN),
        select_weight,
    )


def solution(mesh):
    placed = (
        P("dp", "ctx", "mp"),
        P("dp", "ctx", "mp"),
        P("dp"),
        P(None, "dp", "mp"),
        P(None, None, "dp", "mp"),
        P("dp", None, ("ctx", "mp")),
        P("dp", None, ("ctx", "mp")),
        P(None, None, "dp", ("ctx", "mp")),
        P(None, "dp", ("ctx", "mp")),
        P(None, ("ctx", "mp")),
        P(("ctx", "mp")),
        P(None, ("ctx", "mp")),
        P(("ctx", "mp")),
        P(None, ("ctx", "mp")),
        P("dp"),
        P("dp"),
    )
    return jax.shard_map(
        on_device,
        mesh=mesh,
        in_specs=placed,
        out_specs=(P(None, "dp", "mp"), P(None, "dp", ("ctx", "mp"))),
        check_vma=False,
    )
```

```python
import functools

import jax
import jax.numpy as jnp
from jax import lax
from jax.experimental import pallas as pl
from jax.experimental.pallas import tpu as pltpu
from jax.sharding import PartitionSpec as P

HEAD = 128
NEGATIVE = -1e30
SCALE = HEAD**-0.5
MESH = pl.DeviceIdType.MESH
F32 = jnp.float32
BF16 = jnp.bfloat16

N_DP = 16
N_CTX = 8
N_MP = 4
SLOTS = 4
BLOCK = 256
CHAN = 512
CHUNKS = CHAN // 128
STATE = 16

ROW_Q = 0
ROW_F = 32
ROW_M = 40
MSG = 48
ROW_S = 48
ROWS = 56

LOAD_ORDER = (1, 2, 5, 6, 9, 10, 7, 11, 12, 0, 15, 3, 4, 8, 13, 14)


def kernel(*refs):
    operands, (att_ref, mam_ref), rest = refs[:16], refs[16:18], refs[18:]
    local, in_sem, rest = rest[:16], rest[16], rest[17:]
    run(operands, local, in_sem, att_ref, mam_ref, *rest)


def run(
    operands,
    local,
    in_sem,
    att_ref,
    mam_ref,
    table_out,
    table_in,
    member,
    rows_new,
    rows_old,
    ask_out,
    ask_in,
    size_out,
    size_in,
    moved,
    moved_sizes,
    asked,
    fresh_rows,
    filt,
    sel_out,
    sel_mp,
    sel_sum,
    sel_ctx,
    part_out,
    part_in,
    fin_out,
    fin_in,
    scan_rows,
    mam_rows,
    mam_out,
    mam_in,
    ans_out,
    ans_in,
    back_rows,
    send_sem,
    recv_sem,
):
    (lengths, target_group, target_slot, key_ref, value_ref, query_ref, fresh_ref, recent_ref) = local[:8]
    (state_ref, inputs_ref, steps_ref, taps_ref, bias_ref, decay_ref, skip_ref, select_ref) = local[8:]
    loads = [pltpu.make_async_copy(operands[k], local[k], in_sem.at[k]) for k in range(16)]
    for k in LOAD_ORDER:
        loads[k].start()

    d = lax.axis_index("dp")
    c = lax.axis_index("ctx")
    m = lax.axis_index("mp")

    def over_dp(fn):
        def body(k, carry):
            fn(lax.rem(d + k, N_DP))
            return carry

        lax.fori_loop(1, N_DP, body, 0)

    def over_ctx(fn):
        def body(k, carry):
            fn(lax.rem(c + k, N_CTX))
            return carry

        lax.fori_loop(1, N_CTX, body, 0)

    def over_mp(fn):
        def body(k, carry):
            fn(lax.rem(m + k, N_MP))
            return carry

        lax.fori_loop(1, N_MP, body, 0)

    def send(src, dst, phase, device):
        pltpu.make_async_remote_copy(
            src_ref=src,
            dst_ref=dst,
            send_sem=send_sem.at[phase],
            recv_sem=recv_sem.at[phase],
            device_id=device,
            device_id_type=MESH,
        ).start()

    def arrived(buffer, phase, count):
        part = buffer.at[pl.ds(0, count)]
        pltpu.make_async_copy(part, part, recv_sem.at[phase]).wait()

    def sent(buffer, phase, count):
        part = buffer.at[pl.ds(0, count)]
        pltpu.make_async_copy(part, part, send_sem.at[phase]).wait()

    barrier = pltpu.get_barrier_semaphore()
    over_dp(lambda p: pl.semaphore_signal(barrier, inc=1, device_id={"dp": p}, device_id_type=MESH))
    over_ctx(lambda p: pl.semaphore_signal(barrier, inc=1, device_id={"ctx": p}, device_id_type=MESH))
    over_mp(lambda p: pl.semaphore_signal(barrier, inc=1, device_id={"mp": p}, device_id_type=MESH))

    loads[1].wait()
    loads[2].wait()
    lane = lax.broadcasted_iota(jnp.int32, (1, 128), 1)
    landing = jnp.full((1, 128), -1, jnp.int32)
    for s in range(SLOTS):
        landing = jnp.where(lane == s, target_group[s] * SLOTS + target_slot[s], landing)
    table_out[0] = landing
    table_in[d] = landing
    pl.semaphore_wait(barrier, (N_DP - 1) + (N_CTX - 1) + (N_MP - 1))

    over_dp(lambda p: send(table_out.at[0], table_in.at[d], 0, {"dp": p}))

    for k in (5, 6, 9, 10):
        loads[k].wait()
    for t in (1, 2):
        q = query_ref[t].astype(F32)
        for j in range(16):
            rows_new[pl.ds(ROW_Q + (t - 1) * 16 + j, SLOTS, stride=ROWS), :] = q[:, j * 128 : (j + 1) * 128]
        for kv in range(2):
            f = fresh_ref[t, kv].astype(F32)
            for h in range(2):
                rows_new[pl.ds(ROW_F + (t - 1) * 4 + kv * 2 + h, SLOTS, stride=ROWS), :] = f[:, h * 128 : (h + 1) * 128]
        x = inputs_ref[t, 0].astype(F32)
        for ch in range(CHUNKS):
            rows_new[pl.ds(ROW_M + (t - 1) * 4 + ch, SLOTS, stride=ROWS), :] = x[:, ch * 128 : (ch + 1) * 128]
        x = steps_ref[t]
        for ch in range(CHUNKS):
            rows_new[pl.ds(ROW_S + (t - 1) * 4 + ch, SLOTS, stride=ROWS), :] = x[:, ch * 128 : (ch + 1) * 128]
    q = query_ref[0].astype(F32)
    for j in range(16):
        rows_old[pl.ds(j, SLOTS, stride=24), :] = q[:, j * 128 : (j + 1) * 128]
    for kv in range(2):
        f = fresh_ref[0, kv].astype(F32)
        for h in range(2):
            rows_old[pl.ds(16 + kv * 2 + h, SLOTS, stride=24), :] = f[:, h * 128 : (h + 1) * 128]

    arrived(table_in, 0, N_DP - 1)
    table = table_in[...].reshape(N_DP, 128)
    for i in range(SLOTS):
        hit = jnp.where(table == d * SLOTS + i, 1.0, 0.0).astype(F32)
        member[i] = jnp.broadcast_to(jnp.max(hit, axis=1, keepdims=True), (N_DP, 128))

    def chosen(p, first, last):
        total = rows_new[first:last, :] * member[0, pl.ds(p, 1), :]
        for i in range(1, SLOTS):
            total += rows_new[i * ROWS + first : i * ROWS + last, :] * member[i, pl.ds(p, 1), :]
        return total

    def ask_one(p):
        ask_out[p] = chosen(p, 0, MSG).astype(BF16)
        send(ask_out.at[p], ask_in.at[d], 1, {"dp": p})

    over_dp(ask_one)
    ask_in[d] = chosen(d, 0, MSG).astype(BF16)

    def size_one(p):
        size_out[p] = chosen(p, ROW_S, ROWS)
        send(size_out.at[p], size_in.at[d], 8, {"dp": p})

    over_dp(size_one)
    size_in[d] = chosen(d, ROW_S, ROWS)

    for k in (7, 11, 12):
        loads[k].wait()
    taps = taps_ref[...].astype(F32)
    bias = bias_ref[...]
    window = [recent_ref[k].astype(F32) for k in range(3)] + [inputs_ref[0, 0].astype(F32)]

    def filtered(parts):
        total = parts[0] * taps[0:1, :]
        for k in range(1, 4):
            total += parts[k] * taps[k : k + 1, :]
        total += bias
        return (total * jax.nn.sigmoid(total)).astype(BF16).astype(F32)

    filt[0, 0:SLOTS, :] = filtered(window)

    arrived(ask_in, 1, N_DP - 1)
    for s in range(SLOTS):
        moved[s * MSG : (s + 1) * MSG, :] = ask_in[target_group[s]].astype(F32)

    def lined_up(ref, row, stride):
        return jnp.concatenate([ref[pl.ds(row + ch, SLOTS, stride=stride), :] for ch in range(CHUNKS)], axis=1)

    for t in (1, 2):
        window = window[1:] + [lined_up(moved, ROW_M + (t - 1) * 4, MSG)]
        filt[t, 0:SLOTS, :] = filtered(window)
    loads[15].wait()
    weight = select_ref[...]
    weight = jnp.concatenate([weight] * SLOTS, axis=0)
    own = lax.broadcasted_iota(jnp.int32, (8, 128), 1) // 32 == lax.broadcasted_iota(jnp.int32, (8, 128), 0)
    picks = []
    for t in range(3):
        product = lax.dot_general(
            filt[t].astype(BF16), weight, (((1,), (1,)), ((), ())), preferred_element_type=F32
        )
        picks.append(jnp.sum(jnp.where(own, product, 0.0), axis=0, keepdims=True))
    sel_out[0] = jnp.concatenate(picks + [jnp.zeros((5, 128), F32)], axis=0)
    sel_mp[m] = sel_out[0]
    over_mp(lambda p: send(sel_out.at[0], sel_mp.at[m], 2, {"mp": p}))

    for k in (0, 3, 4):
        loads[k].wait()
    positions = lax.broadcasted_iota(jnp.int32, (1, BLOCK), 1) + c * BLOCK
    lanes = lax.broadcasted_iota(jnp.int32, (24, 128), 1)
    for s in range(SLOTS):
        usable = positions < lengths[s]
        for h in range(2):
            unit = s * 2 + h
            asks = jnp.concatenate(
                [rows_old[s * 24 + h * 8 : s * 24 + h * 8 + 8, :]]
                + [moved[s * MSG + ROW_Q + t * 16 + h * 8 : s * MSG + ROW_Q + t * 16 + h * 8 + 8, :] for t in range(2)],
                axis=0,
            )
            asked[unit] = asks
            fresh_rows[unit] = jnp.concatenate(
                [rows_old[s * 24 + 16 + h : s * 24 + 17 + h, :]]
                + [moved[s * MSG + ROW_F + t * 4 + h : s * MSG + ROW_F + t * 4 + h + 1, :] for t in range(2)]
                + [rows_old[s * 24 + 18 + h : s * 24 + 19 + h, :]]
                + [moved[s * MSG + ROW_F + t * 4 + 2 + h : s * MSG + ROW_F + t * 4 + 3 + h, :] for t in range(2)]
                + [jnp.zeros((2, 128), F32)],
                axis=0,
            )
            keys = key_ref[s, :, h * 128 : (h + 1) * 128]
            values = value_ref[s, :, h * 128 : (h + 1) * 128]
            scores = (
                lax.dot_general(asks.astype(BF16), keys, (((1,), (1,)), ((), ())), preferred_element_type=F32) * SCALE
            )
            scores = jnp.where(usable, scores, NEGATIVE)
            top = jnp.max(scores, axis=1, keepdims=True).astype(BF16).astype(F32)
            weights = jnp.where(usable, jnp.exp(scores - top), 0.0)
            total = jnp.sum(weights, axis=1, keepdims=True)
            mixed = jnp.dot(weights.astype(BF16), values, preferred_element_type=F32)
            high = total.astype(BF16).astype(F32)
            stats = jnp.where(lanes == 0, top, jnp.where(lanes == 1, high, total - high))
            part_out[unit] = jnp.concatenate([mixed, stats], axis=0).astype(BF16)
    part_in[c] = part_out[c]
    over_ctx(lambda p: send(part_out.at[p], part_in.at[c], 3, {"ctx": p}))

    arrived(sel_mp, 2, N_MP - 1)
    total = sel_mp[0]
    for k in range(1, N_MP):
        total += sel_mp[k]
    sel_sum[0] = total
    sel_ctx[c] = total
    over_ctx(lambda p: send(sel_sum.at[0], sel_ctx.at[c], 4, {"ctx": p}))

    arrived(part_in, 3, N_CTX - 1)
    asks = asked[c]
    fresh = fresh_rows[c]
    step_of = lax.broadcasted_iota(jnp.int32, (24, 1), 0) // 8
    parts = [part_in[k].astype(F32) for k in range(N_CTX)]
    tops = [part[24:48, 0:1] for part in parts]
    overall = tops[0]
    for k in range(1, N_CTX):
        overall = jnp.maximum(overall, tops[k])
    recents = []
    for u in range(3):
        score = jnp.sum(asks * fresh[u : u + 1, :], axis=1, keepdims=True) * SCALE
        score = jnp.where(step_of >= u, score, NEGATIVE)
        recents.append(score)
        overall = jnp.maximum(overall, score)
    numerator = jnp.zeros((24, 128), F32)
    denominator = jnp.zeros((24, 1), F32)
    for k in range(N_CTX):
        keep = jnp.exp(tops[k] - overall)
        numerator += parts[k][0:24, :] * keep
        denominator += (parts[k][24:48, 1:2] + parts[k][24:48, 2:3]) * keep
    for u in range(3):
        keep = jnp.where(step_of >= u, jnp.exp(recents[u] - overall), 0.0)
        numerator += fresh[3 + u : 4 + u, :] * keep
        denominator += keep
    done = jnp.concatenate([numerator / denominator, jnp.zeros((8, 128), F32)], axis=0).astype(BF16)
    fin_out[0] = done
    fin_in[c] = done
    over_ctx(lambda p: send(fin_out.at[0], fin_in.at[c], 5, {"ctx": p}))

    arrived(sel_ctx, 4, N_CTX - 1)
    total = sel_ctx[0]
    for k in range(1, N_CTX):
        total += sel_ctx[k]
    columns = jnp.transpose(total)
    arrived(size_in, 8, N_DP - 1)
    for s in range(SLOTS):
        moved_sizes[s * 8 : (s + 1) * 8, :] = size_in[target_group[s]]
    for k in (8, 13, 14):
        loads[k].wait()
    rates = jnp.exp(decay_ref[...])
    sizes = [steps_ref[0]] + [lined_up(moved_sizes, (t - 1) * 4, 8) for t in (1, 2)]
    inputs = [filt[t, 0:SLOTS, :] for t in range(3)]

    def gated(result, t):
        gate = inputs_ref[t, 1].astype(F32)
        return (result * (gate * jax.nn.sigmoid(gate))).astype(BF16)

    for s in range(SLOTS):
        hidden = state_ref[s]
        for t in range(3):
            size = sizes[t][s : s + 1, :]
            into = columns[s * 32 : s * 32 + 16, t : t + 1]
            out = columns[s * 32 + 16 : s * 32 + 32, t : t + 1]
            hidden = jnp.exp(-size * rates) * hidden + into * (size * inputs[t][s : s + 1, :])
            scan_rows[t, s : s + 1, :] = jnp.sum(out * hidden, axis=0, keepdims=True)
    for t in range(3):
        result = scan_rows[t, 0:SLOTS, :] + skip_ref[...] * inputs[t]
        if t == 0:
            mam_ref[0] = gated(result, 0)
        else:
            for ch in range(CHUNKS):
                mam_rows[pl.ds((t - 1) * 4 + ch, SLOTS, stride=8), :] = result[:, ch * 128 : (ch + 1) * 128]

    def leaves(s, p):
        return jnp.where(target_group[s] == p, 1.0, 0.0).astype(F32)

    def mam_message(p):
        total = mam_rows[0:8, :] * leaves(0, p)
        for s in range(1, SLOTS):
            total += mam_rows[s * 8 : (s + 1) * 8, :] * leaves(s, p)
        return total

    def mam_one(p):
        mam_out[p] = mam_message(p)
        send(mam_out.at[p], mam_in.at[d], 6, {"dp": p})

    over_dp(mam_one)
    mam_in[d] = mam_message(d)

    arrived(fin_in, 5, N_CTX - 1)
    finished = [fin_in[k].astype(F32) for k in range(N_CTX)]
    for s in range(SLOTS):
        for h in range(2):
            back_rows[s * 32 + h * 16 : s * 32 + h * 16 + 16, :] = finished[s * 2 + h][8:24, :]

    def ans_message(p):
        total = back_rows[0:32, :] * leaves(0, p)
        for s in range(1, SLOTS):
            total += back_rows[s * 32 : (s + 1) * 32, :] * leaves(s, p)
        return total.astype(BF16)

    def ans_one(p):
        ans_out[p] = ans_message(p)
        send(ans_out.at[p], ans_in.at[d], 7, {"dp": p})

    over_dp(ans_one)
    ans_in[d] = ans_message(d)
    for s in range(SLOTS):
        for h in range(2):
            rows_old[s * 24 + h * 8 : s * 24 + h * 8 + 8, :] = finished[s * 2 + h][0:8, :]
    for j in range(16):
        att_ref[0, :, j * 128 : (j + 1) * 128] = rows_old[pl.ds(j, SLOTS, stride=24), :].astype(BF16)

    arrived(mam_in, 6, N_DP - 1)
    for i in range(SLOTS):
        total = mam_in[0] * member[i, 0:1, :]
        for g in range(1, N_DP):
            total += mam_in[g] * member[i, g : g + 1, :]
        mam_rows[i * 8 : (i + 1) * 8, :] = total
    for t in (1, 2):
        mam_ref[t] = gated(lined_up(mam_rows, (t - 1) * 4, 8), t)
    arrived(ans_in, 7, N_DP - 1)
    for i in range(SLOTS):
        total = ans_in[0].astype(F32) * member[i, 0:1, :]
        for g in range(1, N_DP):
            total += ans_in[g].astype(F32) * member[i, g : g + 1, :]
        back_rows[i * 32 : (i + 1) * 32, :] = total
    for t in (1, 2):
        for h in range(2):
            for j in range(8):
                att_ref[t, :, (h * 8 + j) * 128 : (h * 8 + j + 1) * 128] = back_rows[
                    pl.ds(h * 16 + (t - 1) * 8 + j, SLOTS, stride=32), :
                ].astype(BF16)

    sent(table_in, 0, N_DP - 1)
    sent(ask_out, 1, N_DP - 1)
    sent(size_out, 8, N_DP - 1)
    sent(sel_mp, 2, N_MP - 1)
    sent(part_out, 3, N_CTX - 1)
    sent(sel_ctx, 4, N_CTX - 1)
    sent(fin_in, 5, N_CTX - 1)
    sent(mam_out, 6, N_DP - 1)
    sent(ans_out, 7, N_DP - 1)


def on_device(
    key_cache,
    value_cache,
    lengths,
    queries,
    fresh_pairs,
    recent_inputs,
    scan_state,
    mamba_inputs,
    step_sizes,
    filter_taps,
    filter_bias,
    decay_logs,
    skip_gain,
    select_weight,
    target_group,
    target_slot,
):
    vmem = pl.BlockSpec(memory_space=pltpu.VMEM)
    operands = (
        lengths,
        target_group,
        target_slot,
        key_cache,
        value_cache,
        queries,
        fresh_pairs,
        jnp.swapaxes(recent_inputs, 0, 1),
        scan_state,
        mamba_inputs,
        step_sizes,
        filter_taps,
        filter_bias.reshape(1, CHAN),
        decay_logs,
        skip_gain.reshape(1, CHAN),
        select_weight,
    )
    return pl.pallas_call(
        kernel,
        out_shape=(
            jax.ShapeDtypeStruct((3, SLOTS, 2048), BF16),
            jax.ShapeDtypeStruct((3, SLOTS, CHAN), BF16),
        ),
        in_specs=[pl.BlockSpec(memory_space=pltpu.HBM)] * 16,
        out_specs=(vmem, vmem),
        scratch_shapes=[pltpu.SMEM((SLOTS,), jnp.int32)] * 3
        + [pltpu.VMEM(x.shape, x.dtype) for x in operands[3:]]
        + [
            pltpu.SemaphoreType.DMA((16,)),
            pltpu.VMEM((1, 1, 128), jnp.int32),
            pltpu.VMEM((N_DP, 1, 128), jnp.int32),
            pltpu.VMEM((SLOTS, N_DP, 128), F32),
            pltpu.VMEM((SLOTS * ROWS, 128), F32),
            pltpu.VMEM((SLOTS * 24, 128), F32),
            pltpu.VMEM((N_DP, MSG, 128), BF16),
            pltpu.VMEM((N_DP, MSG, 128), BF16),
            pltpu.VMEM((N_DP, 8, 128), F32),
            pltpu.VMEM((N_DP, 8, 128), F32),
            pltpu.VMEM((SLOTS * MSG, 128), F32),
            pltpu.VMEM((SLOTS * 8, 128), F32),
            pltpu.VMEM((8, 24, 128), F32),
            pltpu.VMEM((8, 8, 128), F32),
            pltpu.VMEM((3, 8, CHAN), F32),
            pltpu.VMEM((1, 8, 128), F32),
            pltpu.VMEM((N_MP, 8, 128), F32),
            pltpu.VMEM((1, 8, 128), F32),
            pltpu.VMEM((N_CTX, 8, 128), F32),
            pltpu.VMEM((N_CTX, 48, 128), BF16),
            pltpu.VMEM((N_CTX, 48, 128), BF16),
            pltpu.VMEM((1, 32, 128), BF16),
            pltpu.VMEM((N_CTX, 32, 128), BF16),
            pltpu.VMEM((3, 8, CHAN), F32),
            pltpu.VMEM((SLOTS * 8, 128), F32),
            pltpu.VMEM((N_DP, 8, 128), F32),
            pltpu.VMEM((N_DP, 8, 128), F32),
            pltpu.VMEM((N_DP, 32, 128), BF16),
            pltpu.VMEM((N_DP, 32, 128), BF16),
            pltpu.VMEM((SLOTS * 32, 128), F32),
            pltpu.SemaphoreType.DMA((9,)),
            pltpu.SemaphoreType.DMA((9,)),
        ],
        compiler_params=pltpu.CompilerParams(
            collective_id=0, has_side_effects=True, vmem_limit_bytes=60 * 2**20
        ),
    )(*operands)


def solution(mesh):
    placed = (
        P("dp", "ctx", "mp"),
        P("dp", "ctx", "mp"),
        P("dp"),
        P(None, "dp", "mp"),
        P(None, None, "dp", "mp"),
        P("dp", None, ("ctx", "mp")),
        P("dp", None, ("ctx", "mp")),
        P(None, None, "dp", ("ctx", "mp")),
        P(None, "dp", ("ctx", "mp")),
        P(None, ("ctx", "mp")),
        P(("ctx", "mp")),
        P(None, ("ctx", "mp")),
        P(("ctx", "mp")),
        P(None, ("ctx", "mp")),
        P("dp"),
        P("dp"),
    )
    return jax.shard_map(
        on_device,
        mesh=mesh,
        in_specs=placed,
        out_specs=(P(None, "dp", "mp"), P(None, "dp", ("ctx", "mp"))),
        check_vma=False,
    )
```

```python
import functools

import jax
import jax.numpy as jnp
from jax import lax
from jax.experimental import pallas as pl
from jax.experimental.pallas import tpu as pltpu
from jax.sharding import PartitionSpec as P

HEAD = 128
NEGATIVE = -1e30
SCALE = HEAD**-0.5
MESH = pl.DeviceIdType.MESH
F32 = jnp.float32
BF16 = jnp.bfloat16

N_DP = 16
N_CTX = 8
N_MP = 4
SLOTS = 4
BLOCK = 256
CHAN = 512
CHUNKS = CHAN // 128
STATE = 16

ROW_Q = 0
ROW_F = 32
ROW_M = 40
ROW_S = 48
ROWS = 56

LOAD_ORDER = (1, 2, 5, 6, 9, 10, 7, 11, 12, 0, 15, 3, 4, 8, 13, 14)


def kernel(*refs):
    operands, (att_ref, mam_ref), rest = refs[:16], refs[16:18], refs[18:]
    local, in_sem, rest = rest[:16], rest[16], rest[17:]
    run(operands, local, in_sem, att_ref, mam_ref, *rest)


def run(
    operands,
    local,
    in_sem,
    att_ref,
    mam_ref,
    table_out,
    table_in,
    member,
    rows_new,
    rows_old,
    ask_out,
    ask_in,
    new_out,
    new_in,
    size_out,
    size_in,
    moved,
    moved_sizes,
    asked,
    fresh_rows,
    filt,
    sel_out,
    sel_mp,
    sel_sum,
    sel_ctx,
    part_out,
    part_in,
    fin_out,
    fin_in,
    one_out,
    one_in,
    scan_rows,
    mam_rows,
    mam_out,
    mam_in,
    ans_out,
    ans_in,
    back_rows,
    send_sem,
    recv_sem,
):
    (lengths, target_group, target_slot, key_ref, value_ref, query_ref, fresh_ref, recent_ref) = local[:8]
    (state_ref, inputs_ref, steps_ref, taps_ref, bias_ref, decay_ref, skip_ref, select_ref) = local[8:]
    loads = [pltpu.make_async_copy(operands[k], local[k], in_sem.at[k]) for k in range(16)]
    for k in LOAD_ORDER:
        loads[k].start()

    d = lax.axis_index("dp")
    c = lax.axis_index("ctx")
    m = lax.axis_index("mp")

    def over_dp(fn):
        def body(k, carry):
            away = N_DP // 2 + jnp.where(k % 2 == 1, -((k + 1) // 2), k // 2)
            fn(lax.rem(d + away, N_DP))
            return carry

        lax.fori_loop(0, N_DP - 1, body, 0)

    def over_ctx(fn):
        def body(k, carry):
            away = N_CTX // 2 + jnp.where(k % 2 == 1, -((k + 1) // 2), k // 2)
            fn(lax.rem(c + away, N_CTX))
            return carry

        lax.fori_loop(0, N_CTX - 1, body, 0)

    def over_mp(fn):
        def body(k, carry):
            away = N_MP // 2 + jnp.where(k % 2 == 1, -((k + 1) // 2), k // 2)
            fn(lax.rem(m + away, N_MP))
            return carry

        lax.fori_loop(0, N_MP - 1, body, 0)

    def send(src, dst, phase, device):
        pltpu.make_async_remote_copy(
            src_ref=src,
            dst_ref=dst,
            send_sem=send_sem.at[phase],
            recv_sem=recv_sem.at[phase],
            device_id=device,
            device_id_type=MESH,
        ).start()

    def arrived(buffer, phase, count):
        part = buffer.at[pl.ds(0, count)]
        pltpu.make_async_copy(part, part, recv_sem.at[phase]).wait()

    def sent(buffer, phase, count):
        part = buffer.at[pl.ds(0, count)]
        pltpu.make_async_copy(part, part, send_sem.at[phase]).wait()

    barrier = pltpu.get_barrier_semaphore()
    over_dp(lambda p: pl.semaphore_signal(barrier, inc=1, device_id={"dp": p}, device_id_type=MESH))
    over_ctx(lambda p: pl.semaphore_signal(barrier, inc=1, device_id={"ctx": p}, device_id_type=MESH))
    over_mp(lambda p: pl.semaphore_signal(barrier, inc=1, device_id={"mp": p}, device_id_type=MESH))

    loads[1].wait()
    loads[2].wait()
    lane = lax.broadcasted_iota(jnp.int32, (1, 128), 1)
    landing = jnp.full((1, 128), -1, jnp.int32)
    for s in range(SLOTS):
        landing = jnp.where(lane == s, target_group[s] * SLOTS + target_slot[s], landing)
    table_out[0] = landing
    table_in[d] = landing
    pl.semaphore_wait(barrier, (N_DP - 1) + (N_CTX - 1) + (N_MP - 1))

    over_dp(lambda p: send(table_out.at[0], table_in.at[d], 0, {"dp": p}))

    for k in (5, 6, 9, 10):
        loads[k].wait()
    for t in (1, 2):
        q = query_ref[t].astype(F32)
        for j in range(16):
            rows_new[pl.ds(ROW_Q + (t - 1) * 16 + j, SLOTS, stride=ROWS), :] = q[:, j * 128 : (j + 1) * 128]
        for kv in range(2):
            f = fresh_ref[t, kv].astype(F32)
            for h in range(2):
                rows_new[pl.ds(ROW_F + (t - 1) * 4 + kv * 2 + h, SLOTS, stride=ROWS), :] = f[:, h * 128 : (h + 1) * 128]
        x = inputs_ref[t, 0].astype(F32)
        for ch in range(CHUNKS):
            rows_new[pl.ds(ROW_M + (t - 1) * 4 + ch, SLOTS, stride=ROWS), :] = x[:, ch * 128 : (ch + 1) * 128]
        x = steps_ref[t]
        for ch in range(CHUNKS):
            rows_new[pl.ds(ROW_S + (t - 1) * 4 + ch, SLOTS, stride=ROWS), :] = x[:, ch * 128 : (ch + 1) * 128]
    q = query_ref[0].astype(F32)
    for j in range(16):
        rows_old[pl.ds(j, SLOTS, stride=24), :] = q[:, j * 128 : (j + 1) * 128]
    for kv in range(2):
        f = fresh_ref[0, kv].astype(F32)
        for h in range(2):
            rows_old[pl.ds(16 + kv * 2 + h, SLOTS, stride=24), :] = f[:, h * 128 : (h + 1) * 128]

    arrived(table_in, 0, N_DP - 1)
    table = table_in[...].reshape(N_DP, 128)
    for i in range(SLOTS):
        hit = jnp.where(table == d * SLOTS + i, 1.0, 0.0).astype(F32)
        member[i] = jnp.broadcast_to(jnp.max(hit, axis=1, keepdims=True), (N_DP, 128))

    def chosen(p, first, last):
        total = rows_new[first:last, :] * member[0, pl.ds(p, 1), :]
        for i in range(1, SLOTS):
            total += rows_new[i * ROWS + first : i * ROWS + last, :] * member[i, pl.ds(p, 1), :]
        return total

    def message(first, last, out, into, phase):
        def one(p):
            out[p] = chosen(p, first, last).astype(out.dtype)
            send(out.at[p], into.at[d], phase, {"dp": p})

        over_dp(one)
        into[d] = chosen(d, first, last).astype(out.dtype)

    message(ROW_Q, ROW_F, ask_out, ask_in, 1)
    message(ROW_F, ROW_S, new_out, new_in, 8)
    message(ROW_S, ROWS, size_out, size_in, 9)

    for k in (7, 11, 12):
        loads[k].wait()
    taps = taps_ref[...].astype(F32)
    bias = bias_ref[...]
    window = [recent_ref[k].astype(F32) for k in range(3)] + [inputs_ref[0, 0].astype(F32)]

    def filtered(parts):
        total = parts[0] * taps[0:1, :]
        for k in range(1, 4):
            total += parts[k] * taps[k : k + 1, :]
        total += bias
        return (total * jax.nn.sigmoid(total)).astype(BF16).astype(F32)

    filt[0, 0:SLOTS, :] = filtered(window)

    for k in (0, 3, 4, 15):
        loads[k].wait()
    positions = lax.broadcasted_iota(jnp.int32, (24, BLOCK), 1) + c * BLOCK
    weight = select_ref[...]
    weight = jnp.concatenate([weight] * SLOTS, axis=0)

    arrived(ask_in, 1, N_DP - 1)
    for s in range(SLOTS):
        queries = ask_in[target_group[s]].astype(F32)
        for h in range(2):
            asked[s * 2 + h] = jnp.concatenate(
                [rows_old[s * 24 + h * 8 : s * 24 + h * 8 + 8, :]]
                + [queries[t * 16 + h * 8 : t * 16 + h * 8 + 8, :] for t in range(2)],
                axis=0,
            )
    units = [(s, h) for s in range(SLOTS) for h in range(2)]
    scores = [
        lax.dot_general(
            asked[s * 2 + h].astype(BF16),
            key_ref[s, :, h * 128 : (h + 1) * 128],
            (((1,), (1,)), ((), ())),
            preferred_element_type=F32,
        )
        * SCALE
        for s, h in units
    ]
    usable = [positions < lengths[s] for s, h in units]
    scores = [jnp.where(usable[k], scores[k], NEGATIVE) for k in range(8)]
    tops = [jnp.max(x, axis=1, keepdims=True).astype(BF16).astype(F32) for x in scores]
    weights = [jnp.where(usable[k], jnp.exp(scores[k] - tops[k]), 0.0) for k in range(8)]
    totals = [jnp.sum(x, axis=1, keepdims=True) for x in weights]
    mixed = [
        jnp.dot(weights[s * 2 + h].astype(BF16), value_ref[s, :, h * 128 : (h + 1) * 128], preferred_element_type=F32)
        for s, h in units
    ]
    lanes = lax.broadcasted_iota(jnp.int32, (24, 128), 1)
    for k in range(8):
        high = totals[k].astype(BF16).astype(F32)
        stats = jnp.where(lanes == 0, tops[k], jnp.where(lanes == 1, high, totals[k] - high))
        part_out[k] = jnp.concatenate([mixed[k], stats], axis=0).astype(BF16)
    part_in[c] = part_out[c]
    over_ctx(lambda p: send(part_out.at[p], part_in.at[c], 3, {"ctx": p}))

    arrived(new_in, 8, N_DP - 1)
    for s in range(SLOTS):
        moved[s * 16 : s * 16 + 16, :] = new_in[target_group[s]].astype(F32)

    def lined_up(ref, row, stride):
        return jnp.concatenate([ref[pl.ds(row + ch, SLOTS, stride=stride), :] for ch in range(CHUNKS)], axis=1)

    for t in (1, 2):
        window = window[1:] + [lined_up(moved, 8 + (t - 1) * 4, 16)]
        filt[t, 0:SLOTS, :] = filtered(window)
    own = lax.broadcasted_iota(jnp.int32, (8, 128), 1) // 32 == lax.broadcasted_iota(jnp.int32, (8, 128), 0)
    picks = []
    for t in range(3):
        product = lax.dot_general(
            filt[t].astype(BF16), weight, (((1,), (1,)), ((), ())), preferred_element_type=F32
        )
        picks.append(jnp.sum(jnp.where(own, product, 0.0), axis=0, keepdims=True))
    sel_out[0] = jnp.concatenate(picks + [jnp.zeros((5, 128), F32)], axis=0)
    sel_mp[m] = sel_out[0]
    over_mp(lambda p: send(sel_out.at[0], sel_mp.at[m], 2, {"mp": p}))

    for s in range(SLOTS):
        for h in range(2):
            fresh_rows[s * 2 + h] = jnp.concatenate(
                [rows_old[s * 24 + 16 + h : s * 24 + 17 + h, :]]
                + [moved[s * 16 + t * 4 + h : s * 16 + t * 4 + h + 1, :] for t in range(2)]
                + [rows_old[s * 24 + 18 + h : s * 24 + 19 + h, :]]
                + [moved[s * 16 + t * 4 + 2 + h : s * 16 + t * 4 + 3 + h, :] for t in range(2)]
                + [jnp.zeros((2, 128), F32)],
                axis=0,
            )

    arrived(sel_mp, 2, N_MP - 1)
    total = sel_mp[0]
    for k in range(1, N_MP):
        total += sel_mp[k]
    sel_sum[0] = total
    sel_ctx[c] = total
    over_ctx(lambda p: send(sel_sum.at[0], sel_ctx.at[c], 4, {"ctx": p}))

    arrived(part_in, 3, N_CTX - 1)
    asks = asked[c]
    fresh = fresh_rows[c]
    step_of = lax.broadcasted_iota(jnp.int32, (24, 1), 0) // 8
    parts = [part_in[k].astype(F32) for k in range(N_CTX)]
    tops = [part[24:48, 0:1] for part in parts]
    overall = tops[0]
    for k in range(1, N_CTX):
        overall = jnp.maximum(overall, tops[k])
    recents = []
    for u in range(3):
        score = jnp.sum(asks * fresh[u : u + 1, :], axis=1, keepdims=True) * SCALE
        score = jnp.where(step_of >= u, score, NEGATIVE)
        recents.append(score)
        overall = jnp.maximum(overall, score)
    numerator = jnp.zeros((24, 128), F32)
    denominator = jnp.zeros((24, 1), F32)
    for k in range(N_CTX):
        keep = jnp.exp(tops[k] - overall)
        numerator += parts[k][0:24, :] * keep
        denominator += (parts[k][24:48, 1:2] + parts[k][24:48, 2:3]) * keep
    for u in range(3):
        keep = jnp.where(step_of >= u, jnp.exp(recents[u] - overall), 0.0)
        numerator += fresh[3 + u : 4 + u, :] * keep
        denominator += keep
    done = numerator / denominator
    fin_out[0] = done[8:24, :].astype(BF16)
    fin_in[c] = done[8:24, :].astype(BF16)
    over_ctx(lambda p: send(fin_out.at[0], fin_in.at[c], 5, {"ctx": p}))
    one_out[0] = done[0:8, :]
    one_in[c] = done[0:8, :]
    over_ctx(lambda p: send(one_out.at[0], one_in.at[c], 10, {"ctx": p}))

    arrived(sel_ctx, 4, N_CTX - 1)
    total = sel_ctx[0]
    for k in range(1, N_CTX):
        total += sel_ctx[k]
    columns = jnp.transpose(total)
    arrived(size_in, 9, N_DP - 1)
    for s in range(SLOTS):
        moved_sizes[s * 8 : (s + 1) * 8, :] = size_in[target_group[s]]
    for k in (8, 13, 14):
        loads[k].wait()
    rates = jnp.exp(decay_ref[...])
    sizes = [steps_ref[0]] + [lined_up(moved_sizes, (t - 1) * 4, 8) for t in (1, 2)]
    inputs = [filt[t, 0:SLOTS, :] for t in range(3)]

    def gated(result, t):
        gate = inputs_ref[t, 1].astype(F32)
        return (result * (gate * jax.nn.sigmoid(gate))).astype(BF16)

    for s in range(SLOTS):
        hidden = state_ref[s]
        for t in range(3):
            size = sizes[t][s : s + 1, :]
            into = columns[s * 32 : s * 32 + 16, t : t + 1]
            out = columns[s * 32 + 16 : s * 32 + 32, t : t + 1]
            hidden = jnp.exp(-size * rates) * hidden + into * (size * inputs[t][s : s + 1, :])
            scan_rows[t, s : s + 1, :] = jnp.sum(out * hidden, axis=0, keepdims=True)
    for t in range(3):
        result = scan_rows[t, 0:SLOTS, :] + skip_ref[...] * inputs[t]
        if t == 0:
            mam_ref[0] = gated(result, 0)
        else:
            for ch in range(CHUNKS):
                mam_rows[pl.ds((t - 1) * 4 + ch, SLOTS, stride=8), :] = result[:, ch * 128 : (ch + 1) * 128]

    def leaves(s, p):
        return jnp.where(target_group[s] == p, 1.0, 0.0).astype(F32)

    def mam_message(p):
        total = mam_rows[0:8, :] * leaves(0, p)
        for s in range(1, SLOTS):
            total += mam_rows[s * 8 : (s + 1) * 8, :] * leaves(s, p)
        return total

    def mam_one(p):
        mam_out[p] = mam_message(p)
        send(mam_out.at[p], mam_in.at[d], 6, {"dp": p})

    over_dp(mam_one)
    mam_in[d] = mam_message(d)

    arrived(fin_in, 5, N_CTX - 1)
    for k in range(N_CTX):
        back_rows[k * 16 : k * 16 + 16, :] = fin_in[k].astype(F32)

    def ans_message(p):
        total = back_rows[0:32, :] * leaves(0, p)
        for s in range(1, SLOTS):
            total += back_rows[s * 32 : (s + 1) * 32, :] * leaves(s, p)
        return total.astype(BF16)

    def ans_one(p):
        ans_out[p] = ans_message(p)
        send(ans_out.at[p], ans_in.at[d], 7, {"dp": p})

    over_dp(ans_one)
    ans_in[d] = ans_message(d)
    arrived(one_in, 10, N_CTX - 1)
    for s in range(SLOTS):
        for h in range(2):
            rows_old[s * 24 + h * 8 : s * 24 + h * 8 + 8, :] = one_in[s * 2 + h]
    for j in range(16):
        att_ref[0, :, j * 128 : (j + 1) * 128] = rows_old[pl.ds(j, SLOTS, stride=24), :].astype(BF16)

    arrived(mam_in, 6, N_DP - 1)
    for i in range(SLOTS):
        total = mam_in[0] * member[i, 0:1, :]
        for g in range(1, N_DP):
            total += mam_in[g] * member[i, g : g + 1, :]
        mam_rows[i * 8 : (i + 1) * 8, :] = total
    for t in (1, 2):
        mam_ref[t] = gated(lined_up(mam_rows, (t - 1) * 4, 8), t)
    arrived(ans_in, 7, N_DP - 1)
    for i in range(SLOTS):
        total = ans_in[0].astype(F32) * member[i, 0:1, :]
        for g in range(1, N_DP):
            total += ans_in[g].astype(F32) * member[i, g : g + 1, :]
        back_rows[i * 32 : (i + 1) * 32, :] = total
    for t in (1, 2):
        for h in range(2):
            for j in range(8):
                att_ref[t, :, (h * 8 + j) * 128 : (h * 8 + j + 1) * 128] = back_rows[
                    pl.ds(h * 16 + (t - 1) * 8 + j, SLOTS, stride=32), :
                ].astype(BF16)

    sent(table_in, 0, N_DP - 1)
    sent(ask_out, 1, N_DP - 1)
    sent(new_out, 8, N_DP - 1)
    sent(size_out, 9, N_DP - 1)
    sent(sel_mp, 2, N_MP - 1)
    sent(part_out, 3, N_CTX - 1)
    sent(sel_ctx, 4, N_CTX - 1)
    sent(fin_in, 5, N_CTX - 1)
    sent(one_in, 10, N_CTX - 1)
    sent(mam_out, 6, N_DP - 1)
    sent(ans_out, 7, N_DP - 1)


def on_device(
    key_cache,
    value_cache,
    lengths,
    queries,
    fresh_pairs,
    recent_inputs,
    scan_state,
    mamba_inputs,
    step_sizes,
    filter_taps,
    filter_bias,
    decay_logs,
    skip_gain,
    select_weight,
    target_group,
    target_slot,
):
    vmem = pl.BlockSpec(memory_space=pltpu.VMEM)
    operands = (
        lengths,
        target_group,
        target_slot,
        key_cache,
        value_cache,
        queries,
        fresh_pairs,
        jnp.swapaxes(recent_inputs, 0, 1),
        scan_state,
        mamba_inputs,
        step_sizes,
        filter_taps,
        filter_bias.reshape(1, CHAN),
        decay_logs,
        skip_gain.reshape(1, CHAN),
        select_weight,
    )
    operands = tuple(pltpu.with_memory_space_constraint(x, pltpu.HBM) for x in operands)
    return pl.pallas_call(
        kernel,
        out_shape=(
            jax.ShapeDtypeStruct((3, SLOTS, 2048), BF16),
            jax.ShapeDtypeStruct((3, SLOTS, CHAN), BF16),
        ),
        in_specs=[pl.BlockSpec(memory_space=pltpu.HBM)] * 16,
        out_specs=(vmem, vmem),
        scratch_shapes=[pltpu.SMEM((SLOTS,), jnp.int32)] * 3
        + [pltpu.VMEM(x.shape, x.dtype) for x in operands[3:]]
        + [
            pltpu.SemaphoreType.DMA((16,)),
            pltpu.VMEM((1, 1, 128), jnp.int32),
            pltpu.VMEM((N_DP, 1, 128), jnp.int32),
            pltpu.VMEM((SLOTS, N_DP, 128), F32),
            pltpu.VMEM((SLOTS * ROWS, 128), F32),
            pltpu.VMEM((SLOTS * 24, 128), F32),
            pltpu.VMEM((N_DP, 32, 128), BF16),
            pltpu.VMEM((N_DP, 32, 128), BF16),
            pltpu.VMEM((N_DP, 16, 128), BF16),
            pltpu.VMEM((N_DP, 16, 128), BF16),
            pltpu.VMEM((N_DP, 8, 128), F32),
            pltpu.VMEM((N_DP, 8, 128), F32),
            pltpu.VMEM((SLOTS * 16, 128), F32),
            pltpu.VMEM((SLOTS * 8, 128), F32),
            pltpu.VMEM((8, 24, 128), F32),
            pltpu.VMEM((8, 8, 128), F32),
            pltpu.VMEM((3, 8, CHAN), F32),
            pltpu.VMEM((1, 8, 128), F32),
            pltpu.VMEM((N_MP, 8, 128), F32),
            pltpu.VMEM((1, 8, 128), F32),
            pltpu.VMEM((N_CTX, 8, 128), F32),
            pltpu.VMEM((N_CTX, 48, 128), BF16),
            pltpu.VMEM((N_CTX, 48, 128), BF16),
            pltpu.VMEM((1, 16, 128), BF16),
            pltpu.VMEM((N_CTX, 16, 128), BF16),
            pltpu.VMEM((1, 8, 128), F32),
            pltpu.VMEM((N_CTX, 8, 128), F32),
            pltpu.VMEM((3, 8, CHAN), F32),
            pltpu.VMEM((SLOTS * 8, 128), F32),
            pltpu.VMEM((N_DP, 8, 128), F32),
            pltpu.VMEM((N_DP, 8, 128), F32),
            pltpu.VMEM((N_DP, 32, 128), BF16),
            pltpu.VMEM((N_DP, 32, 128), BF16),
            pltpu.VMEM((SLOTS * 32, 128), F32),
            pltpu.SemaphoreType.DMA((11,)),
            pltpu.SemaphoreType.DMA((11,)),
        ],
        compiler_params=pltpu.CompilerParams(
            collective_id=0, has_side_effects=True, vmem_limit_bytes=32 * 2**20
        ),
    )(*operands)


def solution(mesh):
    placed = (
        P("dp", "ctx", "mp"),
        P("dp", "ctx", "mp"),
        P("dp"),
        P(None, "dp", "mp"),
        P(None, None, "dp", "mp"),
        P("dp", None, ("ctx", "mp")),
        P("dp", None, ("ctx", "mp")),
        P(None, None, "dp", ("ctx", "mp")),
        P(None, "dp", ("ctx", "mp")),
        P(None, ("ctx", "mp")),
        P(("ctx", "mp")),
        P(None, ("ctx", "mp")),
        P(("ctx", "mp")),
        P(None, ("ctx", "mp")),
        P("dp"),
        P("dp"),
    )
    return jax.shard_map(
        on_device,
        mesh=mesh,
        in_specs=placed,
        out_specs=(P(None, "dp", "mp"), P(None, "dp", ("ctx", "mp"))),
        check_vma=False,
    )
```

```python
import functools

import jax
import jax.numpy as jnp
from jax import lax
from jax.experimental import pallas as pl
from jax.experimental.pallas import tpu as pltpu
from jax.sharding import PartitionSpec as P

HEAD = 128
NEGATIVE = -1e30
SCALE = HEAD**-0.5
MESH = pl.DeviceIdType.MESH
F32 = jnp.float32
BF16 = jnp.bfloat16

N_DP = 16
N_CTX = 8
N_MP = 4
SLOTS = 4
UNITS = 8
BLOCK = 256
CHAN = 512
CHUNKS = CHAN // 128

ROW_Q = 0
ROW_M = 32
ROW_S = 40
ROWS = 48

FIRST_LOADS = (1, 2)
LATER_LOADS = (5, 6, 9, 10, 0, 3, 4, 7, 11, 12, 15, 8, 13, 14)

TABLE, ASK, ONE, NEW, PART, SELECT_MP, SELECT_CTX, ONE_DONE, DONE, MAMBA, ANSWER = range(11)


def kernel(*refs):
    operands, (att_ref, mam_ref), rest = refs[:16], refs[16:18], refs[18:]
    local, in_sem, rest = rest[:16], rest[16], rest[17:]
    run(operands, local, in_sem, att_ref, mam_ref, *rest)


def run(
    operands,
    local,
    in_sem,
    att_ref,
    mam_ref,
    table_out,
    table_in,
    member,
    rows_new,
    rows_old,
    ask_out,
    ask_in,
    new_out,
    new_in,
    moved,
    asked_one,
    asked,
    asked_new,
    fresh_one,
    fresh_new,
    mixed_rows,
    stats_rows,
    filt,
    sel_out,
    sel_mp,
    sel_sum,
    sel_ctx,
    one_part_out,
    one_part_in,
    part_out,
    part_in,
    fin_out,
    fin_in,
    one_out,
    one_in,
    scan_rows,
    mam_rows,
    mam_out,
    mam_in,
    ans_out,
    ans_in,
    back_rows,
    all_rows,
    send_sem,
    recv_sem,
):
    (lengths, target_group, target_slot, key_ref, value_ref, query_ref, fresh_ref, recent_ref) = local[:8]
    (state_ref, inputs_ref, steps_ref, taps_ref, bias_ref, decay_ref, skip_ref, select_ref) = local[8:]
    loads = [pltpu.make_async_copy(operands[k], local[k], in_sem.at[k]) for k in range(16)]
    for k in FIRST_LOADS:
        loads[k].start()

    d = lax.axis_index("dp")
    c = lax.axis_index("ctx")
    m = lax.axis_index("mp")

    def far_first(here, count, fn):
        def body(k, carry):
            step = (k + 1) // 2
            p = here + count // 2 + jnp.where(k == 2 * step, step, -step)
            fn(jnp.where(p >= count, p - count, p))
            return carry

        lax.fori_loop(0, count - 1, body, 0)

    def over_dp(fn):
        far_first(d, N_DP, fn)

    def over_ctx(fn):
        far_first(c, N_CTX, fn)

    def over_mp(fn):
        far_first(m, N_MP, fn)

    def send(src, dst, phase, device):
        pltpu.make_async_remote_copy(
            src_ref=src,
            dst_ref=dst,
            send_sem=send_sem.at[phase],
            recv_sem=recv_sem.at[phase],
            device_id=device,
            device_id_type=MESH,
        ).start()

    def arrived(buffer, phase, count):
        part = buffer.at[pl.ds(0, count)]
        pltpu.make_async_copy(part, part, recv_sem.at[phase]).wait()

    def sent(buffer, phase, count):
        part = buffer.at[pl.ds(0, count)]
        pltpu.make_async_copy(part, part, send_sem.at[phase]).wait()

    barrier = pltpu.get_barrier_semaphore()

    def greet(device):
        pl.semaphore_signal(barrier, inc=1, device_id=device, device_id_type=MESH)

    over_dp(lambda p: greet({"dp": p}))
    over_ctx(lambda p: greet({"ctx": p}))
    over_mp(lambda p: greet({"mp": p}))
    for k in LATER_LOADS:
        loads[k].start()

    loads[1].wait()
    loads[2].wait()
    lane = lax.broadcasted_iota(jnp.int32, (1, 128), 1)
    landing = jnp.full((1, 128), -1, jnp.int32)
    for s in range(SLOTS):
        landing = jnp.where(lane == s, target_group[s] * SLOTS + target_slot[s], landing)
    table_out[0] = landing
    table_in[d] = landing
    pl.semaphore_wait(barrier, (N_DP - 1) + (N_CTX - 1) + (N_MP - 1))

    over_dp(lambda p: send(table_out.at[0], table_in.at[d], TABLE, {"dp": p}))

    for k in (5, 6, 9, 10):
        loads[k].wait()
    for t in (1, 2):
        q = query_ref[t].astype(F32)
        for j in range(16):
            rows_new[pl.ds(ROW_Q + j * 2 + t - 1, SLOTS, stride=ROWS), :] = q[:, j * 128 : (j + 1) * 128]
        x = inputs_ref[t, 0].astype(F32)
        for ch in range(CHUNKS):
            rows_new[pl.ds(ROW_M + (t - 1) * 4 + ch, SLOTS, stride=ROWS), :] = x[:, ch * 128 : (ch + 1) * 128]
        x = steps_ref[t]
        for ch in range(CHUNKS):
            rows_new[pl.ds(ROW_S + (t - 1) * 4 + ch, SLOTS, stride=ROWS), :] = x[:, ch * 128 : (ch + 1) * 128]
    q = query_ref[0].astype(F32)
    for j in range(16):
        rows_old[pl.ds(j, SLOTS, stride=24), :] = q[:, j * 128 : (j + 1) * 128]
    for kv in range(2):
        f = fresh_ref[0, kv].astype(F32)
        for h in range(2):
            rows_old[pl.ds(16 + kv * 2 + h, SLOTS, stride=24), :] = f[:, h * 128 : (h + 1) * 128]

    units = [(s, h) for s in range(SLOTS) for h in range(2)]

    def attention(questions, rows):
        positions = lax.broadcasted_iota(jnp.int32, (rows, BLOCK), 1) + c * BLOCK
        lanes = lax.broadcasted_iota(jnp.int32, (rows, 128), 1)
        scores = [
            lax.dot_general(
                questions[k],
                key_ref[s, :, h * 128 : (h + 1) * 128],
                (((1,), (1,)), ((), ())),
                preferred_element_type=F32,
            )
            * SCALE
            for k, (s, h) in enumerate(units)
        ]
        usable = [positions < lengths[s] for s, h in units]
        scores = [jnp.where(usable[k], scores[k], NEGATIVE) for k in range(UNITS)]
        tops = [jnp.max(x, axis=1, keepdims=True).astype(BF16).astype(F32) for x in scores]
        weights = [jnp.where(usable[k], jnp.exp(scores[k] - tops[k]), 0.0) for k in range(UNITS)]
        totals = [jnp.sum(x, axis=1, keepdims=True) for x in weights]
        mixed = [
            jnp.dot(weights[k].astype(BF16), value_ref[s, :, h * 128 : (h + 1) * 128], preferred_element_type=F32)
            for k, (s, h) in enumerate(units)
        ]
        stats = []
        for k in range(UNITS):
            high = totals[k].astype(BF16).astype(F32)
            stats.append(jnp.where(lanes == 0, tops[k], jnp.where(lanes == 1, high, totals[k] - high)))
        return mixed, stats

    for s in range(SLOTS):
        for h in range(2):
            asked_one[s * 2 + h] = rows_old[s * 24 + h * 8 : s * 24 + h * 8 + 8, :]
            fresh_one[s * 2 + h] = jnp.concatenate(
                [
                    rows_old[s * 24 + 16 + h : s * 24 + 17 + h, :],
                    rows_old[s * 24 + 18 + h : s * 24 + 19 + h, :],
                    jnp.zeros((6, 128), F32),
                ],
                axis=0,
            )
    for k in (0, 3, 4):
        loads[k].wait()
    mixed, stats = attention([asked_one[k].astype(BF16) for k in range(UNITS)], 8)
    for k in range(UNITS):
        one_part_out[k] = jnp.concatenate([mixed[k], stats[k]], axis=0).astype(BF16)
    one_part_in[c] = one_part_out[c]
    over_ctx(lambda p: send(one_part_out.at[p], one_part_in.at[c], ONE, {"ctx": p}))

    arrived(table_in, TABLE, N_DP - 1)
    table = table_in[...].reshape(N_DP, 128)
    for i in range(SLOTS):
        hit = jnp.where(table == d * SLOTS + i, 1.0, 0.0).astype(F32)
        member[i] = jnp.broadcast_to(jnp.max(hit, axis=1, keepdims=True), (N_DP, 128))

    def chosen(p, first, last):
        total = rows_new[first:last, :] * member[0, pl.ds(p, 1), :]
        for i in range(1, SLOTS):
            total += rows_new[i * ROWS + first : i * ROWS + last, :] * member[i, pl.ds(p, 1), :]
        return total

    def message(first, last, out, into, phase):
        def one(p):
            out[p] = chosen(p, first, last).astype(out.dtype)
            send(out.at[p], into.at[d], phase, {"dp": p})

        over_dp(one)
        into[d] = chosen(d, first, last).astype(out.dtype)

    message(ROW_Q, ROW_M, ask_out, ask_in, ASK)
    message(ROW_M, ROWS, new_out, new_in, NEW)

    for s in range(SLOTS):
        for k in range(N_CTX):
            asked_new[s * N_CTX + k] = rows_new[s * ROWS + k * 4 : s * ROWS + k * 4 + 4, :]
    for t in (1, 2):
        for kv in range(2):
            f = fresh_ref[t, kv].astype(F32)
            for s in range(SLOTS):
                for h in range(2):
                    fresh_new[s * 2 + h, (t - 1) * 2 + kv : (t - 1) * 2 + kv + 1, :] = f[s : s + 1, h * 128 : (h + 1) * 128]
    kv_head = c // (N_CTX // 2)

    def pair_rows(ref, row):
        return jnp.concatenate(
            [jnp.broadcast_to(ref[s * 2 + kv_head, row : row + 1, :], (4, 128)) for s in range(SLOTS)], axis=0
        )

    def head_rows(ref):
        return jnp.concatenate([ref[s * N_CTX + c] for s in range(SLOTS)], axis=0)

    def score_of(questions, keys):
        return jnp.sum(questions * keys, axis=1, keepdims=True) * SCALE

    own_asks = head_rows(asked_new)
    last_step = lax.broadcasted_iota(jnp.int32, (16, 1), 0) % 2 == 1
    second_score = score_of(own_asks, pair_rows(fresh_new, 0))
    third_score = jnp.where(last_step, score_of(own_asks, pair_rows(fresh_new, 2)), NEGATIVE)
    second_value = pair_rows(fresh_new, 1)
    third_value = pair_rows(fresh_new, 3)

    for k in (7, 11, 12, 15):
        loads[k].wait()
    taps = taps_ref[...].astype(F32)
    bias = bias_ref[...]
    window = [recent_ref[k].astype(F32) for k in range(3)] + [inputs_ref[0, 0].astype(F32)]

    def filtered(parts):
        total = parts[0] * taps[0:1, :]
        for k in range(1, 4):
            total += parts[k] * taps[k : k + 1, :]
        total += bias
        return (total * jax.nn.sigmoid(total)).astype(BF16).astype(F32)

    filt[0, 0:SLOTS, :] = filtered(window)
    weight = select_ref[...]
    weight = jnp.concatenate([weight] * SLOTS, axis=0)

    arrived(ask_in, ASK, N_DP - 1)
    questions = []
    for s in range(SLOTS):
        queries = ask_in[target_group[s]]
        questions += [queries[0:16, :], queries[16:32, :]]
        queries = queries.astype(F32)
        for k in range(N_CTX):
            asked[s * N_CTX + k] = queries[k * 4 : k * 4 + 4, :]
    mixed, stats = attention(questions, 16)
    for k in range(UNITS):
        for j in range(4):
            at = ((k % 2) * 4 + j) * 16 + (k // 2) * 4
            mixed_rows[at : at + 4, :] = mixed[k][j * 4 : j * 4 + 4, :]
            stats_rows[at : at + 4, :] = stats[k][j * 4 : j * 4 + 4, :]
    for k in range(N_CTX):
        part_out[k] = jnp.concatenate(
            [mixed_rows[k * 16 : k * 16 + 16, :], stats_rows[k * 16 : k * 16 + 16, :]], axis=0
        ).astype(BF16)
    part_in[c] = part_out[c]
    over_ctx(lambda p: send(part_out.at[p], part_in.at[c], PART, {"ctx": p}))

    arrived(new_in, NEW, N_DP - 1)
    for s in range(SLOTS):
        moved[s * 16 : s * 16 + 16, :] = new_in[target_group[s]].astype(F32)

    def lined_up(ref, row, stride):
        return jnp.concatenate([ref[pl.ds(row + ch, SLOTS, stride=stride), :] for ch in range(CHUNKS)], axis=1)

    for t in (1, 2):
        window = window[1:] + [lined_up(moved, (t - 1) * 4, 16)]
        filt[t, 0:SLOTS, :] = filtered(window)
    own = lax.broadcasted_iota(jnp.int32, (8, 128), 1) // 32 == lax.broadcasted_iota(jnp.int32, (8, 128), 0)
    picks = []
    for t in range(3):
        product = lax.dot_general(
            filt[t].astype(BF16), weight, (((1,), (1,)), ((), ())), preferred_element_type=F32
        )
        picks.append(jnp.sum(jnp.where(own, product, 0.0), axis=0, keepdims=True))
    sel_out[0] = jnp.concatenate(picks + [jnp.zeros((5, 128), F32)], axis=0)
    sel_mp[m] = sel_out[0]
    over_mp(lambda p: send(sel_out.at[0], sel_mp.at[m], SELECT_MP, {"mp": p}))

    def finish(part_in, rows, score, value):
        parts = [part_in[k].astype(F32) for k in range(N_CTX)]
        tops = [part[rows : 2 * rows, 0:1] for part in parts]
        overall = score
        for k in range(N_CTX):
            overall = jnp.maximum(overall, tops[k])
        denominator = jnp.exp(score - overall)
        numerator = value * denominator
        for k in range(N_CTX):
            keep = jnp.exp(tops[k] - overall)
            numerator += parts[k][0:rows, :] * keep
            denominator += (parts[k][rows : 2 * rows, 1:2] + parts[k][rows : 2 * rows, 2:3]) * keep
        return numerator / denominator, overall, denominator

    own_pair = fresh_one[c]
    arrived(one_part_in, ONE, N_CTX - 1)
    one_out[0] = finish(one_part_in, 8, score_of(asked_one[c], own_pair[0:1, :]), own_pair[1:2, :])[0]
    one_in[c] = one_out[0]
    over_ctx(lambda p: send(one_out.at[0], one_in.at[c], ONE_DONE, {"ctx": p}))

    arrived(sel_mp, SELECT_MP, N_MP - 1)
    total = sel_mp[0]
    for k in range(1, N_MP):
        total += sel_mp[k]
    sel_sum[0] = total
    sel_ctx[c] = total
    over_ctx(lambda p: send(sel_sum.at[0], sel_ctx.at[c], SELECT_CTX, {"ctx": p}))

    def leaves(s, p):
        return jnp.where(target_group[s] == p, 1.0, 0.0).astype(F32)

    def returned(rows, p):
        total = rows[0:8, :] * leaves(0, p)
        for s in range(1, SLOTS):
            total += rows[s * 8 : (s + 1) * 8, :] * leaves(s, p)
        return total

    first_score = score_of(head_rows(asked), pair_rows(fresh_one, 0))
    first_value = pair_rows(fresh_one, 1)
    arrived(part_in, PART, N_CTX - 1)
    done, overall, denominator = finish(part_in, 16, first_score, first_value)
    weight_log = jnp.broadcast_to(overall + jnp.log(denominator), (16, 128))
    for s in range(SLOTS):
        back_rows[s * 8 : s * 8 + 4, :] = done[s * 4 : s * 4 + 4, :]
        back_rows[s * 8 + 4 : s * 8 + 8, :] = weight_log[s * 4 : s * 4 + 4, :]

    def ans_one(p):
        ans_out[p] = returned(back_rows, p)
        send(ans_out.at[p], ans_in.at[d], ANSWER, {"dp": p})

    over_dp(ans_one)
    ans_in[d] = returned(back_rows, d)

    for k in (8, 13, 14):
        loads[k].wait()
    rates = jnp.exp(decay_ref[...])
    sizes = [steps_ref[0]] + [lined_up(moved, 8 + (t - 1) * 4, 16) for t in (1, 2)]
    inputs = [filt[t, 0:SLOTS, :] for t in range(3)]

    def gated(result, t):
        gate = inputs_ref[t, 1].astype(F32)
        return (result * (gate * jax.nn.sigmoid(gate))).astype(BF16)

    arrived(sel_ctx, SELECT_CTX, N_CTX - 1)
    total = sel_ctx[0]
    for k in range(1, N_CTX):
        total += sel_ctx[k]
    columns = jnp.transpose(total)
    for s in range(SLOTS):
        hidden = state_ref[s]
        for t in range(3):
            size = sizes[t][s : s + 1, :]
            into = columns[s * 32 : s * 32 + 16, t : t + 1]
            out = columns[s * 32 + 16 : s * 32 + 32, t : t + 1]
            hidden = jnp.exp(-size * rates) * hidden + into * (size * inputs[t][s : s + 1, :])
            scan_rows[t, s : s + 1, :] = jnp.sum(out * hidden, axis=0, keepdims=True)
    for t in range(3):
        result = scan_rows[t, 0:SLOTS, :] + skip_ref[...] * inputs[t]
        if t == 0:
            mam_ref[0] = gated(result, 0)
        else:
            for ch in range(CHUNKS):
                mam_rows[pl.ds((t - 1) * 4 + ch, SLOTS, stride=8), :] = result[:, ch * 128 : (ch + 1) * 128]

    def mam_one(p):
        mam_out[p] = returned(mam_rows, p)
        send(mam_out.at[p], mam_in.at[d], MAMBA, {"dp": p})

    over_dp(mam_one)
    mam_in[d] = returned(mam_rows, d)

    def picked(ref, i):
        total = ref[0] * member[i, 0:1, :]
        for g in range(1, N_DP):
            total += ref[g] * member[i, g : g + 1, :]
        return total

    arrived(ans_in, ANSWER, N_DP - 1)
    found = [picked(ans_in, i) for i in range(SLOTS)]
    cached = jnp.concatenate([x[0:4, :] for x in found], axis=0)
    cached_log = jnp.concatenate([x[4:8, :] for x in found], axis=0)[:, 0:1]
    overall = jnp.maximum(cached_log, jnp.maximum(second_score, third_score))
    keeps = [jnp.exp(cached_log - overall), jnp.exp(second_score - overall)]
    keeps.append(jnp.where(last_step, jnp.exp(third_score - overall), 0.0))
    done = (cached * keeps[0] + second_value * keeps[1] + third_value * keeps[2]) / (keeps[0] + keeps[1] + keeps[2])
    fin_out[0] = done.astype(BF16)
    fin_in[c] = done.astype(BF16)
    over_ctx(lambda p: send(fin_out.at[0], fin_in.at[c], DONE, {"ctx": p}))

    arrived(one_in, ONE_DONE, N_CTX - 1)
    for s in range(SLOTS):
        for h in range(2):
            rows_old[s * 24 + h * 8 : s * 24 + h * 8 + 8, :] = one_in[s * 2 + h]
    for j in range(16):
        att_ref[0, :, j * 128 : (j + 1) * 128] = rows_old[pl.ds(j, SLOTS, stride=24), :].astype(BF16)

    arrived(mam_in, MAMBA, N_DP - 1)
    for i in range(SLOTS):
        mam_rows[i * 8 : (i + 1) * 8, :] = picked(mam_in, i)
    for t in (1, 2):
        mam_ref[t] = gated(lined_up(mam_rows, (t - 1) * 4, 8), t)

    sent(table_in, TABLE, N_DP - 1)
    sent(ask_out, ASK, N_DP - 1)
    sent(new_out, NEW, N_DP - 1)
    sent(one_part_out, ONE, N_CTX - 1)
    sent(sel_mp, SELECT_MP, N_MP - 1)
    sent(sel_ctx, SELECT_CTX, N_CTX - 1)
    sent(part_out, PART, N_CTX - 1)
    sent(ans_out, ANSWER, N_DP - 1)
    sent(one_in, ONE_DONE, N_CTX - 1)
    sent(mam_out, MAMBA, N_DP - 1)

    arrived(fin_in, DONE, N_CTX - 1)
    for k in range(N_CTX):
        all_rows[k * 16 : (k + 1) * 16, :] = fin_in[k].astype(F32)
    for t in (1, 2):
        for j in range(16):
            att_ref[t, :, j * 128 : (j + 1) * 128] = all_rows[
                pl.ds((j // 2) * 16 + (j % 2) * 2 + t - 1, SLOTS, stride=4), :
            ].astype(BF16)
    sent(fin_in, DONE, N_CTX - 1)


def on_device(
    key_cache,
    value_cache,
    lengths,
    queries,
    fresh_pairs,
    recent_inputs,
    scan_state,
    mamba_inputs,
    step_sizes,
    filter_taps,
    filter_bias,
    decay_logs,
    skip_gain,
    select_weight,
    target_group,
    target_slot,
):
    vmem = pl.BlockSpec(memory_space=pltpu.VMEM)
    operands = (
        lengths,
        target_group,
        target_slot,
        key_cache,
        value_cache,
        queries,
        fresh_pairs,
        jnp.swapaxes(recent_inputs, 0, 1),
        scan_state,
        mamba_inputs,
        step_sizes,
        filter_taps,
        filter_bias.reshape(1, CHAN),
        decay_logs,
        skip_gain.reshape(1, CHAN),
        select_weight,
    )
    operands = tuple(pltpu.with_memory_space_constraint(x, pltpu.HBM) for x in operands)
    return pl.pallas_call(
        kernel,
        out_shape=(
            jax.ShapeDtypeStruct((3, SLOTS, 2048), BF16),
            jax.ShapeDtypeStruct((3, SLOTS, CHAN), BF16),
        ),
        in_specs=[pl.BlockSpec(memory_space=pltpu.HBM)] * 16,
        out_specs=(vmem, vmem),
        scratch_shapes=[pltpu.SMEM((SLOTS,), jnp.int32)] * 3
        + [pltpu.VMEM(x.shape, x.dtype) for x in operands[3:]]
        + [
            pltpu.SemaphoreType.DMA((16,)),
            pltpu.VMEM((1, 1, 128), jnp.int32),
            pltpu.VMEM((N_DP, 1, 128), jnp.int32),
            pltpu.VMEM((SLOTS, N_DP, 128), F32),
            pltpu.VMEM((SLOTS * ROWS, 128), F32),
            pltpu.VMEM((SLOTS * 24, 128), F32),
            pltpu.VMEM((N_DP, 32, 128), BF16),
            pltpu.VMEM((N_DP, 32, 128), BF16),
            pltpu.VMEM((N_DP, 16, 128), BF16),
            pltpu.VMEM((N_DP, 16, 128), BF16),
            pltpu.VMEM((SLOTS * 16, 128), F32),
            pltpu.VMEM((UNITS, 8, 128), F32),
            pltpu.VMEM((SLOTS * N_CTX, 4, 128), F32),
            pltpu.VMEM((SLOTS * N_CTX, 4, 128), F32),
            pltpu.VMEM((UNITS, 8, 128), F32),
            pltpu.VMEM((UNITS, 8, 128), F32),
            pltpu.VMEM((N_CTX * 16, 128), F32),
            pltpu.VMEM((N_CTX * 16, 128), F32),
            pltpu.VMEM((3, 8, CHAN), F32),
            pltpu.VMEM((1, 8, 128), F32),
            pltpu.VMEM((N_MP, 8, 128), F32),
            pltpu.VMEM((1, 8, 128), F32),
            pltpu.VMEM((N_CTX, 8, 128), F32),
            pltpu.VMEM((N_CTX, 16, 128), BF16),
            pltpu.VMEM((N_CTX, 16, 128), BF16),
            pltpu.VMEM((N_CTX, 32, 128), BF16),
            pltpu.VMEM((N_CTX, 32, 128), BF16),
            pltpu.VMEM((1, 16, 128), BF16),
            pltpu.VMEM((N_CTX, 16, 128), BF16),
            pltpu.VMEM((1, 8, 128), F32),
            pltpu.VMEM((N_CTX, 8, 128), F32),
            pltpu.VMEM((3, 8, CHAN), F32),
            pltpu.VMEM((SLOTS * 8, 128), F32),
            pltpu.VMEM((N_DP, 8, 128), F32),
            pltpu.VMEM((N_DP, 8, 128), F32),
            pltpu.VMEM((N_DP, 8, 128), F32),
            pltpu.VMEM((N_DP, 8, 128), F32),
            pltpu.VMEM((SLOTS * 8, 128), F32),
            pltpu.VMEM((N_CTX * 16, 128), F32),
            pltpu.SemaphoreType.DMA((11,)),
            pltpu.SemaphoreType.DMA((11,)),
        ],
        compiler_params=pltpu.CompilerParams(
            collective_id=0, has_side_effects=True, vmem_limit_bytes=32 * 2**20
        ),
    )(*operands)


def solution(mesh):
    placed = (
        P("dp", "ctx", "mp"),
        P("dp", "ctx", "mp"),
        P("dp"),
        P(None, "dp", "mp"),
        P(None, None, "dp", "mp"),
        P("dp", None, ("ctx", "mp")),
        P("dp", None, ("ctx", "mp")),
        P(None, None, "dp", ("ctx", "mp")),
        P(None, "dp", ("ctx", "mp")),
        P(None, ("ctx", "mp")),
        P(("ctx", "mp")),
        P(None, ("ctx", "mp")),
        P(("ctx", "mp")),
        P(None, ("ctx", "mp")),
        P("dp"),
        P("dp"),
    )
    return jax.shard_map(
        on_device,
        mesh=mesh,
        in_specs=placed,
        out_specs=(P(None, "dp", "mp"), P(None, "dp", ("ctx", "mp"))),
        check_vma=False,
    )
```

```python
import functools

import jax
import jax.numpy as jnp
from jax import lax
from jax.experimental import pallas as pl
from jax.experimental.pallas import tpu as pltpu
from jax.sharding import PartitionSpec as P

HEAD = 128
NEGATIVE = -1e30
SCALE = HEAD**-0.5
MESH = pl.DeviceIdType.MESH
F32 = jnp.float32
BF16 = jnp.bfloat16

N_DP = 16
N_CTX = 8
N_MP = 4
N_SEL = N_CTX * N_MP
SLOTS = 4
UNITS = 8
BLOCK = 256
CHAN = 512
CHUNKS = CHAN // 128

ROW_M = 0
ROW_S = 8
ROWS = 16

FIRST_LOADS = (1, 2, 5)
LATER_LOADS = (6, 9, 10, 0, 3, 4, 7, 11, 12, 15, 8, 13, 14)

TABLE, ASK, ONE, NEW, PART, SELECT, ONE_DONE, DONE, MAMBA, ANSWER, FORWARD = range(11)


def kernel(*refs):
    operands, (att_ref, mam_ref), rest = refs[:16], refs[16:18], refs[18:]
    local, in_sem, rest = rest[:16], rest[16], rest[17:]
    run(operands, local, in_sem, att_ref, mam_ref, *rest)


def run(
    operands,
    local,
    in_sem,
    att_ref,
    mam_ref,
    table_out,
    table_in,
    member,
    rows_ask,
    rows_new,
    rows_old,
    ask_out,
    ask_in,
    new_out,
    new_in,
    moved,
    asked_one,
    asked,
    asked_new,
    fresh_one,
    fresh_new,
    mixed_rows,
    stats_rows,
    filt,
    sel_out,
    sel_in,
    one_part_out,
    one_part_in,
    part_out,
    part_in,
    fin_out,
    fin_in,
    one_out,
    one_in,
    decays,
    pushed,
    scan_rows,
    mam_rows,
    mam_out,
    mam_in,
    ans_out,
    ans_in,
    back_rows,
    all_rows,
    send_sem,
    recv_sem,
    ask_sem,
):
    (lengths, target_group, target_slot, key_ref, value_ref, query_ref, fresh_ref, recent_ref) = local[:8]
    (state_ref, inputs_ref, steps_ref, taps_ref, bias_ref, decay_ref, skip_ref, select_ref) = local[8:]
    loads = [pltpu.make_async_copy(operands[k], local[k], in_sem.at[k]) for k in range(16)]
    for k in FIRST_LOADS:
        loads[k].start()

    d = lax.axis_index("dp")
    c = lax.axis_index("ctx")
    m = lax.axis_index("mp")
    me = c * N_MP + m
    partner = d + 1 - 2 * (d % 2)

    def far_first(here, count, fn):
        def body(k, carry):
            step = (k + 1) // 2
            p = here + count // 2 + jnp.where(k == 2 * step, step, -step)
            fn(jnp.where(p >= count, p - count, p))
            return carry

        lax.fori_loop(0, count - 1, body, 0)

    def first_started(here, count, fn):
        def body(k, carry):
            fn(k + jnp.where(k >= here, 1, 0))
            return carry

        lax.fori_loop(0, count - 1, body, 0)

    def over_dp(fn):
        far_first(d, N_DP, fn)

    def over_ctx(fn):
        far_first(c, N_CTX, fn)

    def over_mp(fn):
        far_first(m, N_MP, fn)

    def over_sel(fn):
        far_first(me, N_SEL, lambda p: fn({"ctx": p // N_MP, "mp": p % N_MP}))

    def send(src, dst, phase, device):
        pltpu.make_async_remote_copy(
            src_ref=src,
            dst_ref=dst,
            send_sem=send_sem.at[phase],
            recv_sem=recv_sem.at[phase],
            device_id=device,
            device_id_type=MESH,
        ).start()

    def arrived(buffer, phase, count):
        part = buffer.at[pl.ds(0, count)]
        pltpu.make_async_copy(part, part, recv_sem.at[phase]).wait()

    def sent(buffer, phase, count):
        part = buffer.at[pl.ds(0, count)]
        pltpu.make_async_copy(part, part, send_sem.at[phase]).wait()

    barrier = pltpu.get_barrier_semaphore()

    def greet(device):
        pl.semaphore_signal(barrier, inc=1, device_id=device, device_id_type=MESH)

    over_dp(lambda p: greet({"dp": p}))
    over_ctx(lambda p: greet({"ctx": p}))
    over_mp(lambda p: greet({"mp": p}))
    for k in LATER_LOADS:
        loads[k].start()

    loads[1].wait()
    loads[2].wait()
    lane = lax.broadcasted_iota(jnp.int32, (1, 128), 1)
    landing = jnp.full((1, 128), -1, jnp.int32)
    for s in range(SLOTS):
        landing = jnp.where(lane == s, target_group[s] * SLOTS + target_slot[s], landing)
    table_out[0] = landing
    table_in[d] = landing
    loads[5].wait()
    for t in (1, 2):
        q = query_ref[t].astype(F32)
        for j in range(16):
            rows_ask[pl.ds(j * 2 + t - 1, SLOTS, stride=32), :] = q[:, j * 128 : (j + 1) * 128]
    for s in range(SLOTS):
        ask_out[s] = rows_ask[s * 32 : s * 32 + 32, :].astype(BF16)
        ask_in[d, s] = ask_out[s]
    pl.semaphore_wait(barrier, (N_DP - 1) + (N_CTX - 1) + (N_MP - 1))

    over_dp(lambda p: send(table_out.at[0], table_in.at[d], TABLE, {"dp": p}))

    def ask_one(k, carry):
        step = (k + 1) // 2
        p = d + N_DP // 2 + 2 * jnp.where(k == 2 * step, step, -step)
        pltpu.make_async_remote_copy(
            src_ref=ask_out,
            dst_ref=ask_in.at[d],
            send_sem=send_sem.at[ASK],
            recv_sem=ask_sem.at[d // 2],
            device_id={"dp": jnp.where(p >= N_DP, p - N_DP, p)},
            device_id_type=MESH,
        ).start()
        return carry

    lax.fori_loop(0, N_DP // 2 - 1, ask_one, 0)
    send(ask_out, ask_in.at[d], FORWARD, {"dp": partner})

    for k in (6, 9, 10):
        loads[k].wait()
    for t in (1, 2):
        x = inputs_ref[t, 0].astype(F32)
        for ch in range(CHUNKS):
            rows_new[pl.ds(ROW_M + (t - 1) * 4 + ch, SLOTS, stride=ROWS), :] = x[:, ch * 128 : (ch + 1) * 128]
        x = steps_ref[t]
        for ch in range(CHUNKS):
            rows_new[pl.ds(ROW_S + (t - 1) * 4 + ch, SLOTS, stride=ROWS), :] = x[:, ch * 128 : (ch + 1) * 128]
    q = query_ref[0].astype(F32)
    for j in range(16):
        rows_old[pl.ds(j, SLOTS, stride=24), :] = q[:, j * 128 : (j + 1) * 128]
    for kv in range(2):
        f = fresh_ref[0, kv].astype(F32)
        for h in range(2):
            rows_old[pl.ds(16 + kv * 2 + h, SLOTS, stride=24), :] = f[:, h * 128 : (h + 1) * 128]

    units = [(s, h) for s in range(SLOTS) for h in range(2)]

    def attention(questions, rows):
        positions = lax.broadcasted_iota(jnp.int32, (rows, BLOCK), 1) + c * BLOCK
        lanes = lax.broadcasted_iota(jnp.int32, (rows, 128), 1)
        scores = [
            lax.dot_general(
                questions[k],
                key_ref[s, :, h * 128 : (h + 1) * 128],
                (((1,), (1,)), ((), ())),
                preferred_element_type=F32,
            )
            * SCALE
            for k, (s, h) in enumerate(units)
        ]
        usable = [positions < lengths[s] for s, h in units]
        scores = [jnp.where(usable[k], scores[k], NEGATIVE) for k in range(UNITS)]
        tops = [jnp.max(x, axis=1, keepdims=True).astype(BF16).astype(F32) for x in scores]
        weights = [jnp.where(usable[k], jnp.exp(scores[k] - tops[k]), 0.0) for k in range(UNITS)]
        totals = [jnp.sum(x, axis=1, keepdims=True) for x in weights]
        mixed = [
            jnp.dot(weights[k].astype(BF16), value_ref[s, :, h * 128 : (h + 1) * 128], preferred_element_type=F32)
            for k, (s, h) in enumerate(units)
        ]
        stats = []
        for k in range(UNITS):
            high = totals[k].astype(BF16).astype(F32)
            stats.append(jnp.where(lanes == 0, tops[k], jnp.where(lanes == 1, high, totals[k] - high)))
        return mixed, stats

    for s in range(SLOTS):
        for h in range(2):
            asked_one[s * 2 + h] = rows_old[s * 24 + h * 8 : s * 24 + h * 8 + 8, :]
            fresh_one[s * 2 + h] = jnp.concatenate(
                [
                    rows_old[s * 24 + 16 + h : s * 24 + 17 + h, :],
                    rows_old[s * 24 + 18 + h : s * 24 + 19 + h, :],
                    jnp.zeros((6, 128), F32),
                ],
                axis=0,
            )
    for k in (0, 3, 4):
        loads[k].wait()
    mixed, stats = attention([asked_one[k].astype(BF16) for k in range(UNITS)], 8)
    for k in range(UNITS):
        one_part_out[k] = jnp.concatenate([mixed[k], stats[k]], axis=0).astype(BF16)
    one_part_in[c] = one_part_out[c]
    over_ctx(lambda p: send(one_part_out.at[p], one_part_in.at[c], ONE, {"ctx": p}))

    arrived(table_in, TABLE, N_DP - 1)
    table = table_in[...].reshape(N_DP, 128)
    for i in range(SLOTS):
        hit = jnp.where(table == d * SLOTS + i, 1.0, 0.0).astype(F32)
        member[i] = jnp.broadcast_to(jnp.max(hit, axis=1, keepdims=True), (N_DP, 128))

    def chosen(p, first, last):
        total = rows_new[first:last, :] * member[0, pl.ds(p, 1), :]
        for i in range(1, SLOTS):
            total += rows_new[i * ROWS + first : i * ROWS + last, :] * member[i, pl.ds(p, 1), :]
        return total

    def message(first, last, out, into, phase):
        def one(p):
            out[p] = chosen(p, first, last).astype(out.dtype)
            send(out.at[p], into.at[d], phase, {"dp": p})

        over_dp(one)
        into[d] = chosen(d, first, last).astype(out.dtype)

    message(ROW_M, ROWS, new_out, new_in, NEW)

    def forward(k, carry):
        step = k // 2 + 1
        p = d + 2 * jnp.where(k == 2 * step - 2, step, N_DP // 2 - step)
        group = jnp.where(p >= N_DP, p - N_DP, p)
        block = ask_in.at[group]
        pltpu.make_async_copy(block, block, ask_sem.at[group // 2]).wait()
        send(block, block, FORWARD, {"dp": partner})
        return carry

    lax.fori_loop(0, N_DP // 2 - 1, forward, 0)

    for s in range(SLOTS):
        for k in range(N_CTX):
            asked_new[s * N_CTX + k] = rows_ask[s * 32 + k * 4 : s * 32 + k * 4 + 4, :]
    for t in (1, 2):
        for kv in range(2):
            f = fresh_ref[t, kv].astype(F32)
            for s in range(SLOTS):
                for h in range(2):
                    fresh_new[s * 2 + h, (t - 1) * 2 + kv : (t - 1) * 2 + kv + 1, :] = f[s : s + 1, h * 128 : (h + 1) * 128]
    kv_head = c // (N_CTX // 2)

    def pair_rows(ref, row):
        return jnp.concatenate(
            [jnp.broadcast_to(ref[s * 2 + kv_head, row : row + 1, :], (4, 128)) for s in range(SLOTS)], axis=0
        )

    def head_rows(ref):
        return jnp.concatenate([ref[s * N_CTX + c] for s in range(SLOTS)], axis=0)

    def score_of(questions, keys):
        return jnp.sum(questions * keys, axis=1, keepdims=True) * SCALE

    own_asks = head_rows(asked_new)
    last_step = lax.broadcasted_iota(jnp.int32, (16, 1), 0) % 2 == 1
    second_score = score_of(own_asks, pair_rows(fresh_new, 0))
    third_score = jnp.where(last_step, score_of(own_asks, pair_rows(fresh_new, 2)), NEGATIVE)
    second_value = pair_rows(fresh_new, 1)
    third_value = pair_rows(fresh_new, 3)

    for k in (7, 8, 11, 12, 13, 14, 15):
        loads[k].wait()
    taps = taps_ref[...].astype(F32)
    bias = bias_ref[...]
    window = [recent_ref[k].astype(F32) for k in range(3)] + [inputs_ref[0, 0].astype(F32)]

    def filtered(parts):
        total = parts[0] * taps[0:1, :]
        for k in range(1, 4):
            total += parts[k] * taps[k : k + 1, :]
        total += bias
        return (total * jax.nn.sigmoid(total)).astype(BF16).astype(F32)

    filt[0, 0:SLOTS, :] = filtered(window)
    weight = select_ref[...]
    weight = jnp.concatenate([weight] * SLOTS, axis=0)

    arrived(ask_in, FORWARD, N_DP // 2)
    questions = []
    for s in range(SLOTS):
        queries = ask_in[target_group[s], target_slot[s]]
        questions += [queries[0:16, :], queries[16:32, :]]
    mixed, stats = attention(questions, 16)
    for k in range(UNITS):
        for j in range(4):
            at = ((k % 2) * 4 + j) * 16 + (k // 2) * 4
            mixed_rows[at : at + 4, :] = mixed[k][j * 4 : j * 4 + 4, :]
            stats_rows[at : at + 4, :] = stats[k][j * 4 : j * 4 + 4, :]
    for k in range(N_CTX):
        part_out[k] = jnp.concatenate(
            [mixed_rows[k * 16 : k * 16 + 16, :], stats_rows[k * 16 : k * 16 + 16, :]], axis=0
        ).astype(BF16)
    part_in[c] = part_out[c]
    over_ctx(lambda p: send(part_out.at[p], part_in.at[c], PART, {"ctx": p}))
    for s in range(SLOTS):
        queries = ask_in[target_group[s], target_slot[s]].astype(F32)
        for k in range(N_CTX):
            asked[s * N_CTX + k] = queries[k * 4 : k * 4 + 4, :]

    arrived(new_in, NEW, N_DP - 1)
    for s in range(SLOTS):
        moved[s * 16 : s * 16 + 16, :] = new_in[target_group[s]].astype(F32)

    def lined_up(ref, row, stride):
        return jnp.concatenate([ref[pl.ds(row + ch, SLOTS, stride=stride), :] for ch in range(CHUNKS)], axis=1)

    for t in (1, 2):
        window = window[1:] + [lined_up(moved, (t - 1) * 4, 16)]
        filt[t, 0:SLOTS, :] = filtered(window)
    own = lax.broadcasted_iota(jnp.int32, (8, 128), 1) // 32 == lax.broadcasted_iota(jnp.int32, (8, 128), 0)
    picks = []
    for t in range(3):
        product = lax.dot_general(
            filt[t].astype(BF16), weight, (((1,), (1,)), ((), ())), preferred_element_type=F32
        )
        picks.append(jnp.sum(jnp.where(own, product, 0.0), axis=0, keepdims=True))
    arrived(one_part_in, ONE, N_CTX - 1)
    sel_out[0] = jnp.concatenate(picks + [jnp.zeros((5, 128), F32)], axis=0)
    sel_in[me] = sel_out[0]
    over_sel(lambda device: send(sel_out.at[0], sel_in.at[me], SELECT, device))

    def finish(part_in, rows, score, value):
        parts = [part_in[k].astype(F32) for k in range(N_CTX)]
        tops = [part[rows : 2 * rows, 0:1] for part in parts]
        overall = score
        for k in range(N_CTX):
            overall = jnp.maximum(overall, tops[k])
        denominator = jnp.exp(score - overall)
        numerator = value * denominator
        for k in range(N_CTX):
            keep = jnp.exp(tops[k] - overall)
            numerator += parts[k][0:rows, :] * keep
            denominator += (parts[k][rows : 2 * rows, 1:2] + parts[k][rows : 2 * rows, 2:3]) * keep
        return numerator / denominator, overall, denominator

    own_pair = fresh_one[c]
    one_out[0] = finish(one_part_in, 8, score_of(asked_one[c], own_pair[0:1, :]), own_pair[1:2, :])[0]
    one_in[c] = one_out[0]
    over_ctx(lambda p: send(one_out.at[0], one_in.at[c], ONE_DONE, {"ctx": p}))

    rates = jnp.exp(decay_ref[...])
    inputs = [filt[t, 0:SLOTS, :] for t in range(3)]
    for t in range(3):
        sizes = steps_ref[0] if t == 0 else lined_up(moved, 8 + (t - 1) * 4, 16)
        pushed[t, 0:SLOTS, :] = sizes * inputs[t]
        for s in range(SLOTS):
            decays[t, s] = jnp.exp(-sizes[s : s + 1, :] * rates)

    def leaves(s, p):
        return jnp.where(target_group[s] == p, 1.0, 0.0).astype(F32)

    def returned(rows, p):
        total = rows[0:8, :] * leaves(0, p)
        for s in range(1, SLOTS):
            total += rows[s * 8 : (s + 1) * 8, :] * leaves(s, p)
        return total

    first_score = score_of(head_rows(asked), pair_rows(fresh_one, 0))
    first_value = pair_rows(fresh_one, 1)
    arrived(part_in, PART, N_CTX - 1)
    done, overall, denominator = finish(part_in, 16, first_score, first_value)
    weight_log = jnp.broadcast_to(overall + jnp.log(denominator), (16, 128))
    for s in range(SLOTS):
        back_rows[s * 8 : s * 8 + 4, :] = done[s * 4 : s * 4 + 4, :]
        back_rows[s * 8 + 4 : s * 8 + 8, :] = weight_log[s * 4 : s * 4 + 4, :]

    def ans_one(p):
        ans_out[p] = returned(back_rows, p)
        send(ans_out.at[p], ans_in.at[d], ANSWER, {"dp": p})

    first_started(d, N_DP, ans_one)
    ans_in[d] = returned(back_rows, d)

    def gated(result, t):
        gate = inputs_ref[t, 1].astype(F32)
        return (result * (gate * jax.nn.sigmoid(gate))).astype(BF16)

    arrived(sel_in, SELECT, N_SEL - 1)
    total = sel_in[0]
    for k in range(1, N_SEL):
        total += sel_in[k]
    columns = jnp.transpose(total)
    for s in range(SLOTS):
        hidden = state_ref[s]
        for t in range(3):
            into = columns[s * 32 : s * 32 + 16, t : t + 1]
            out = columns[s * 32 + 16 : s * 32 + 32, t : t + 1]
            hidden = decays[t, s] * hidden + into * pushed[t, s : s + 1, :]
            scan_rows[t, s : s + 1, :] = jnp.sum(out * hidden, axis=0, keepdims=True)
    for t in range(3):
        result = scan_rows[t, 0:SLOTS, :] + skip_ref[...] * inputs[t]
        if t == 0:
            mam_ref[0] = gated(result, 0)
        else:
            for ch in range(CHUNKS):
                mam_rows[pl.ds((t - 1) * 4 + ch, SLOTS, stride=8), :] = result[:, ch * 128 : (ch + 1) * 128]

    def mam_one(p):
        mam_out[p] = returned(mam_rows, p)
        send(mam_out.at[p], mam_in.at[d], MAMBA, {"dp": p})

    first_started(d, N_DP, mam_one)
    mam_in[d] = returned(mam_rows, d)

    def picked(ref, i):
        total = ref[0] * member[i, 0:1, :]
        for g in range(1, N_DP):
            total += ref[g] * member[i, g : g + 1, :]
        return total

    arrived(ans_in, ANSWER, N_DP - 1)
    found = [picked(ans_in, i) for i in range(SLOTS)]
    cached = jnp.concatenate([x[0:4, :] for x in found], axis=0)
    cached_log = jnp.concatenate([x[4:8, :] for x in found], axis=0)[:, 0:1]
    overall = jnp.maximum(cached_log, jnp.maximum(second_score, third_score))
    keeps = [jnp.exp(cached_log - overall), jnp.exp(second_score - overall)]
    keeps.append(jnp.where(last_step, jnp.exp(third_score - overall), 0.0))
    done = (cached * keeps[0] + second_value * keeps[1] + third_value * keeps[2]) / (keeps[0] + keeps[1] + keeps[2])
    fin_out[0] = done.astype(BF16)
    fin_in[c] = done.astype(BF16)
    over_ctx(lambda p: send(fin_out.at[0], fin_in.at[c], DONE, {"ctx": p}))

    arrived(one_in, ONE_DONE, N_CTX - 1)
    for s in range(SLOTS):
        for h in range(2):
            rows_old[s * 24 + h * 8 : s * 24 + h * 8 + 8, :] = one_in[s * 2 + h]
    for j in range(16):
        att_ref[0, :, j * 128 : (j + 1) * 128] = rows_old[pl.ds(j, SLOTS, stride=24), :].astype(BF16)

    arrived(mam_in, MAMBA, N_DP - 1)
    for i in range(SLOTS):
        mam_rows[i * 8 : (i + 1) * 8, :] = picked(mam_in, i)
    for t in (1, 2):
        mam_ref[t] = gated(lined_up(mam_rows, (t - 1) * 4, 8), t)

    sent(table_in, TABLE, N_DP - 1)
    sent(ask_in, ASK, N_DP // 2 - 1)
    sent(ask_in, FORWARD, N_DP // 2)
    sent(new_out, NEW, N_DP - 1)
    sent(one_part_out, ONE, N_CTX - 1)
    sent(sel_in, SELECT, N_SEL - 1)
    sent(part_out, PART, N_CTX - 1)
    sent(ans_out, ANSWER, N_DP - 1)
    sent(one_in, ONE_DONE, N_CTX - 1)
    sent(mam_out, MAMBA, N_DP - 1)

    arrived(fin_in, DONE, N_CTX - 1)
    for k in range(N_CTX):
        all_rows[k * 16 : (k + 1) * 16, :] = fin_in[k].astype(F32)
    for t in (1, 2):
        for j in range(16):
            att_ref[t, :, j * 128 : (j + 1) * 128] = all_rows[
                pl.ds((j // 2) * 16 + (j % 2) * 2 + t - 1, SLOTS, stride=4), :
            ].astype(BF16)
    sent(fin_in, DONE, N_CTX - 1)


def on_device(
    key_cache,
    value_cache,
    lengths,
    queries,
    fresh_pairs,
    recent_inputs,
    scan_state,
    mamba_inputs,
    step_sizes,
    filter_taps,
    filter_bias,
    decay_logs,
    skip_gain,
    select_weight,
    target_group,
    target_slot,
):
    vmem = pl.BlockSpec(memory_space=pltpu.VMEM)
    operands = (
        lengths,
        target_group,
        target_slot,
        key_cache,
        value_cache,
        queries,
        fresh_pairs,
        jnp.swapaxes(recent_inputs, 0, 1),
        scan_state,
        mamba_inputs,
        step_sizes,
        filter_taps,
        filter_bias.reshape(1, CHAN),
        decay_logs,
        skip_gain.reshape(1, CHAN),
        select_weight,
    )
    operands = tuple(pltpu.with_memory_space_constraint(x, pltpu.HBM) for x in operands)
    return pl.pallas_call(
        kernel,
        out_shape=(
            jax.ShapeDtypeStruct((3, SLOTS, 2048), BF16),
            jax.ShapeDtypeStruct((3, SLOTS, CHAN), BF16),
        ),
        in_specs=[pl.BlockSpec(memory_space=pltpu.HBM)] * 16,
        out_specs=(vmem, vmem),
        scratch_shapes=[pltpu.SMEM((SLOTS,), jnp.int32)] * 3
        + [pltpu.VMEM(x.shape, x.dtype) for x in operands[3:]]
        + [
            pltpu.SemaphoreType.DMA((16,)),
            pltpu.VMEM((1, 1, 128), jnp.int32),
            pltpu.VMEM((N_DP, 1, 128), jnp.int32),
            pltpu.VMEM((SLOTS, N_DP, 128), F32),
            pltpu.VMEM((SLOTS * 32, 128), F32),
            pltpu.VMEM((SLOTS * ROWS, 128), F32),
            pltpu.VMEM((SLOTS * 24, 128), F32),
            pltpu.VMEM((SLOTS, 32, 128), BF16),
            pltpu.VMEM((N_DP, SLOTS, 32, 128), BF16),
            pltpu.VMEM((N_DP, 16, 128), BF16),
            pltpu.VMEM((N_DP, 16, 128), BF16),
            pltpu.VMEM((SLOTS * 16, 128), F32),
            pltpu.VMEM((UNITS, 8, 128), F32),
            pltpu.VMEM((SLOTS * N_CTX, 4, 128), F32),
            pltpu.VMEM((SLOTS * N_CTX, 4, 128), F32),
            pltpu.VMEM((UNITS, 8, 128), F32),
            pltpu.VMEM((UNITS, 8, 128), F32),
            pltpu.VMEM((N_CTX * 16, 128), F32),
            pltpu.VMEM((N_CTX * 16, 128), F32),
            pltpu.VMEM((3, 8, CHAN), F32),
            pltpu.VMEM((1, 8, 128), F32),
            pltpu.VMEM((N_SEL, 8, 128), F32),
            pltpu.VMEM((N_CTX, 16, 128), BF16),
            pltpu.VMEM((N_CTX, 16, 128), BF16),
            pltpu.VMEM((N_CTX, 32, 128), BF16),
            pltpu.VMEM((N_CTX, 32, 128), BF16),
            pltpu.VMEM((1, 16, 128), BF16),
            pltpu.VMEM((N_CTX, 16, 128), BF16),
            pltpu.VMEM((1, 8, 128), F32),
            pltpu.VMEM((N_CTX, 8, 128), F32),
            pltpu.VMEM((3, SLOTS, 16, CHAN), F32),
            pltpu.VMEM((3, 8, CHAN), F32),
            pltpu.VMEM((3, 8, CHAN), F32),
            pltpu.VMEM((SLOTS * 8, 128), F32),
            pltpu.VMEM((N_DP, 8, 128), F32),
            pltpu.VMEM((N_DP, 8, 128), F32),
            pltpu.VMEM((N_DP, 8, 128), F32),
            pltpu.VMEM((N_DP, 8, 128), F32),
            pltpu.VMEM((SLOTS * 8, 128), F32),
            pltpu.VMEM((N_CTX * 16, 128), F32),
            pltpu.SemaphoreType.DMA((11,)),
            pltpu.SemaphoreType.DMA((11,)),
            pltpu.SemaphoreType.DMA((N_DP // 2,)),
        ],
        compiler_params=pltpu.CompilerParams(
            collective_id=0, has_side_effects=True, vmem_limit_bytes=32 * 2**20
        ),
    )(*operands)


def solution(mesh):
    placed = (
        P("dp", "ctx", "mp"),
        P("dp", "ctx", "mp"),
        P("dp"),
        P(None, "dp", "mp"),
        P(None, None, "dp", "mp"),
        P("dp", None, ("ctx", "mp")),
        P("dp", None, ("ctx", "mp")),
        P(None, None, "dp", ("ctx", "mp")),
        P(None, "dp", ("ctx", "mp")),
        P(None, ("ctx", "mp")),
        P(("ctx", "mp")),
        P(None, ("ctx", "mp")),
        P(("ctx", "mp")),
        P(None, ("ctx", "mp")),
        P("dp"),
        P("dp"),
    )
    return jax.shard_map(
        on_device,
        mesh=mesh,
        in_specs=placed,
        out_specs=(P(None, "dp", "mp"), P(None, "dp", ("ctx", "mp"))),
        check_vma=False,
    )
```

```python
import functools

import jax
import jax.numpy as jnp
from jax import lax
from jax.experimental import pallas as pl
from jax.experimental.pallas import tpu as pltpu
from jax.sharding import PartitionSpec as P

HEAD = 128
NEGATIVE = -1e30
SCALE = HEAD**-0.5
MESH = pl.DeviceIdType.MESH
F32 = jnp.float32
BF16 = jnp.bfloat16

N_DP = 16
N_CTX = 8
N_MP = 4
N_SEL = N_CTX * N_MP
SLOTS = 4
UNITS = 8
BLOCK = 256
CHAN = 512
CHUNKS = CHAN // 128

ROW_M = 0
ROW_S = 8
ROWS = 16

FIRST_LOADS = (1, 2, 5)
LATER_LOADS = (6, 9, 10, 0, 3, 4, 7, 11, 12, 15, 8, 13, 14)

TABLE, ASK, ONE, NEW, PART, SELECT, ONE_DONE, DONE, MAMBA, ANSWER, FORWARD = range(11)


def kernel(*refs):
    operands, (att_ref, mam_ref), rest = refs[:16], refs[16:18], refs[18:]
    local, in_sem, rest = rest[:16], rest[16], rest[17:]
    run(operands, local, in_sem, att_ref, mam_ref, *rest)


def run(
    operands,
    local,
    in_sem,
    att_ref,
    mam_ref,
    table_out,
    table_in,
    member,
    rows_ask,
    rows_new,
    rows_old,
    ask_out,
    ask_in,
    new_out,
    new_in,
    moved,
    asked_one,
    asked,
    asked_new,
    fresh_one,
    fresh_new,
    mixed_rows,
    stats_rows,
    filt,
    sel_out,
    sel_in,
    one_part_out,
    one_part_in,
    part_out,
    part_in,
    fin_out,
    fin_in,
    one_out,
    one_in,
    decays,
    pushed,
    scan_rows,
    mam_rows,
    mam_out,
    mam_in,
    ans_out,
    ans_in,
    back_rows,
    all_rows,
    send_sem,
    recv_sem,
    ask_sem,
):
    (lengths, target_group, target_slot, key_ref, value_ref, query_ref, fresh_ref, recent_ref) = local[:8]
    (state_ref, inputs_ref, steps_ref, taps_ref, bias_ref, decay_ref, skip_ref, select_ref) = local[8:]
    loads = [pltpu.make_async_copy(operands[k], local[k], in_sem.at[k]) for k in range(16)]
    for k in FIRST_LOADS:
        loads[k].start()

    d = lax.axis_index("dp")
    c = lax.axis_index("ctx")
    m = lax.axis_index("mp")
    me = c * N_MP + m
    partner = d + 1 - 2 * (d % 2)

    def far_first(here, count, fn):
        def body(k, carry):
            step = (k + 1) // 2
            p = here + count // 2 + jnp.where(k == 2 * step, step, -step)
            fn(jnp.where(p >= count, p - count, p))
            return carry

        lax.fori_loop(0, count - 1, body, 0)

    def first_started(here, count, fn):
        def body(k, carry):
            fn(k + jnp.where(k >= here, 1, 0))
            return carry

        lax.fori_loop(0, count - 1, body, 0)

    def over_dp(fn):
        far_first(d, N_DP, fn)

    def over_ctx(fn):
        far_first(c, N_CTX, fn)

    def over_mp(fn):
        far_first(m, N_MP, fn)

    def over_sel(fn):
        far_first(me, N_SEL, lambda p: fn({"ctx": p // N_MP, "mp": p % N_MP}))

    def send(src, dst, phase, device):
        pltpu.make_async_remote_copy(
            src_ref=src,
            dst_ref=dst,
            send_sem=send_sem.at[phase],
            recv_sem=recv_sem.at[phase],
            device_id=device,
            device_id_type=MESH,
        ).start()

    def arrived(buffer, phase, count):
        part = buffer.at[pl.ds(0, count)]
        pltpu.make_async_copy(part, part, recv_sem.at[phase]).wait()

    def sent(buffer, phase, count):
        part = buffer.at[pl.ds(0, count)]
        pltpu.make_async_copy(part, part, send_sem.at[phase]).wait()

    barrier = pltpu.get_barrier_semaphore()

    def greet(device):
        pl.semaphore_signal(barrier, inc=1, device_id=device, device_id_type=MESH)

    over_dp(lambda p: greet({"dp": p}))
    over_ctx(lambda p: greet({"ctx": p}))
    over_mp(lambda p: greet({"mp": p}))
    for k in LATER_LOADS:
        loads[k].start()

    loads[1].wait()
    loads[2].wait()
    lane = lax.broadcasted_iota(jnp.int32, (1, 128), 1)
    landing = jnp.full((1, 128), -1, jnp.int32)
    for s in range(SLOTS):
        landing = jnp.where(lane == s, target_group[s] * SLOTS + target_slot[s], landing)
    table_out[0] = landing
    table_in[d] = landing
    loads[5].wait()
    for t in (1, 2):
        q = query_ref[t].astype(F32)
        for j in range(16):
            rows_ask[pl.ds(j * 2 + t - 1, SLOTS, stride=32), :] = q[:, j * 128 : (j + 1) * 128]
    for s in range(SLOTS):
        ask_out[s] = rows_ask[s * 32 : s * 32 + 32, :].astype(BF16)
        ask_in[d, s] = ask_out[s]
    pl.semaphore_wait(barrier, (N_DP - 1) + (N_CTX - 1) + (N_MP - 1))

    over_dp(lambda p: send(table_out.at[0], table_in.at[d], TABLE, {"dp": p}))

    def ask_one(k, carry):
        step = (k + 1) // 2
        p = d + N_DP // 2 + 2 * jnp.where(k == 2 * step, step, -step)
        pltpu.make_async_remote_copy(
            src_ref=ask_out,
            dst_ref=ask_in.at[d],
            send_sem=send_sem.at[ASK],
            recv_sem=ask_sem.at[d // 2],
            device_id={"dp": jnp.where(p >= N_DP, p - N_DP, p)},
            device_id_type=MESH,
        ).start()
        return carry

    lax.fori_loop(0, N_DP // 2 - 1, ask_one, 0)
    send(ask_out, ask_in.at[d], FORWARD, {"dp": partner})

    for k in (6, 9, 10):
        loads[k].wait()
    for t in (1, 2):
        x = inputs_ref[t, 0].astype(F32)
        for ch in range(CHUNKS):
            rows_new[pl.ds(ROW_M + (t - 1) * 4 + ch, SLOTS, stride=ROWS), :] = x[:, ch * 128 : (ch + 1) * 128]
        x = steps_ref[t]
        for ch in range(CHUNKS):
            rows_new[pl.ds(ROW_S + (t - 1) * 4 + ch, SLOTS, stride=ROWS), :] = x[:, ch * 128 : (ch + 1) * 128]
    q = query_ref[0].astype(F32)
    for j in range(16):
        rows_old[pl.ds(j, SLOTS, stride=24), :] = q[:, j * 128 : (j + 1) * 128]
    for kv in range(2):
        f = fresh_ref[0, kv].astype(F32)
        for h in range(2):
            rows_old[pl.ds(16 + kv * 2 + h, SLOTS, stride=24), :] = f[:, h * 128 : (h + 1) * 128]

    units = [(s, h) for s in range(SLOTS) for h in range(2)]

    def attention(questions, rows):
        positions = lax.broadcasted_iota(jnp.int32, (rows, BLOCK), 1) + c * BLOCK
        lanes = lax.broadcasted_iota(jnp.int32, (rows, 128), 1)
        scores = [
            lax.dot_general(
                questions[k],
                key_ref[s, :, h * 128 : (h + 1) * 128],
                (((1,), (1,)), ((), ())),
                preferred_element_type=F32,
            )
            * SCALE
            for k, (s, h) in enumerate(units)
        ]
        usable = [positions < lengths[s] for s, h in units]
        scores = [jnp.where(usable[k], scores[k], NEGATIVE) for k in range(UNITS)]
        tops = [jnp.max(x, axis=1, keepdims=True).astype(BF16).astype(F32) for x in scores]
        weights = [jnp.where(usable[k], jnp.exp(scores[k] - tops[k]), 0.0) for k in range(UNITS)]
        totals = [jnp.sum(x, axis=1, keepdims=True) for x in weights]
        mixed = [
            jnp.dot(weights[k].astype(BF16), value_ref[s, :, h * 128 : (h + 1) * 128], preferred_element_type=F32)
            for k, (s, h) in enumerate(units)
        ]
        stats = []
        for k in range(UNITS):
            high = totals[k].astype(BF16).astype(F32)
            stats.append(jnp.where(lanes == 0, tops[k], jnp.where(lanes == 1, high, totals[k] - high)))
        return mixed, stats

    for s in range(SLOTS):
        for h in range(2):
            asked_one[s * 2 + h] = rows_old[s * 24 + h * 8 : s * 24 + h * 8 + 8, :]
            fresh_one[s * 2 + h] = jnp.concatenate(
                [
                    rows_old[s * 24 + 16 + h : s * 24 + 17 + h, :],
                    rows_old[s * 24 + 18 + h : s * 24 + 19 + h, :],
                    jnp.zeros((6, 128), F32),
                ],
                axis=0,
            )
    for k in (0, 3, 4):
        loads[k].wait()
    mixed, stats = attention([asked_one[k].astype(BF16) for k in range(UNITS)], 8)
    for k in range(UNITS):
        one_part_out[k] = jnp.concatenate([mixed[k], stats[k]], axis=0).astype(BF16)
    one_part_in[c] = one_part_out[c]
    over_ctx(lambda p: send(one_part_out.at[p], one_part_in.at[c], ONE, {"ctx": p}))

    arrived(table_in, TABLE, N_DP - 1)
    table = table_in[...].reshape(N_DP, 128)
    for i in range(SLOTS):
        hit = jnp.where(table == d * SLOTS + i, 1.0, 0.0).astype(F32)
        member[i] = jnp.broadcast_to(jnp.max(hit, axis=1, keepdims=True), (N_DP, 128))

    def chosen(p, first, last):
        total = rows_new[first:last, :] * member[0, pl.ds(p, 1), :]
        for i in range(1, SLOTS):
            total += rows_new[i * ROWS + first : i * ROWS + last, :] * member[i, pl.ds(p, 1), :]
        return total

    def message(first, last, out, into, phase):
        def one(p):
            out[p] = chosen(p, first, last).astype(out.dtype)
            send(out.at[p], into.at[d], phase, {"dp": p})

        over_dp(one)
        into[d] = chosen(d, first, last).astype(out.dtype)

    message(ROW_M, ROWS, new_out, new_in, NEW)

    def forward(k, carry):
        step = k // 2 + 1
        p = d + 2 * jnp.where(k == 2 * step - 2, step, N_DP // 2 - step)
        group = jnp.where(p >= N_DP, p - N_DP, p)
        block = ask_in.at[group]
        pltpu.make_async_copy(block, block, ask_sem.at[group // 2]).wait()
        send(block, block, FORWARD, {"dp": partner})
        return carry

    lax.fori_loop(0, N_DP // 2 - 1, forward, 0)

    for s in range(SLOTS):
        for k in range(N_CTX):
            asked_new[s * N_CTX + k] = rows_ask[s * 32 + k * 4 : s * 32 + k * 4 + 4, :]
    for t in (1, 2):
        for kv in range(2):
            f = fresh_ref[t, kv].astype(F32)
            for s in range(SLOTS):
                for h in range(2):
                    fresh_new[s * 2 + h, (t - 1) * 2 + kv : (t - 1) * 2 + kv + 1, :] = f[s : s + 1, h * 128 : (h + 1) * 128]
    kv_head = c // (N_CTX // 2)

    def pair_rows(ref, row):
        return jnp.concatenate(
            [jnp.broadcast_to(ref[s * 2 + kv_head, row : row + 1, :], (4, 128)) for s in range(SLOTS)], axis=0
        )

    def head_rows(ref):
        return jnp.concatenate([ref[s * N_CTX + c] for s in range(SLOTS)], axis=0)

    def score_of(questions, keys):
        return jnp.sum(questions * keys, axis=1, keepdims=True) * SCALE

    own_asks = head_rows(asked_new)
    last_step = lax.broadcasted_iota(jnp.int32, (16, 1), 0) % 2 == 1
    second_score = score_of(own_asks, pair_rows(fresh_new, 0))
    third_score = jnp.where(last_step, score_of(own_asks, pair_rows(fresh_new, 2)), NEGATIVE)
    second_value = pair_rows(fresh_new, 1)
    third_value = pair_rows(fresh_new, 3)

    for k in (7, 8, 11, 12, 13, 14, 15):
        loads[k].wait()
    taps = taps_ref[...].astype(F32)
    bias = bias_ref[...]
    window = [recent_ref[k].astype(F32) for k in range(3)] + [inputs_ref[0, 0].astype(F32)]

    def filtered(parts):
        total = parts[0] * taps[0:1, :]
        for k in range(1, 4):
            total += parts[k] * taps[k : k + 1, :]
        total += bias
        return (total * jax.nn.sigmoid(total)).astype(BF16).astype(F32)

    filt[0, 0:SLOTS, :] = filtered(window)
    weight = select_ref[...]
    weight = jnp.concatenate([weight] * SLOTS, axis=0)

    arrived(ask_in, FORWARD, N_DP // 2)
    questions = []
    for s in range(SLOTS):
        queries = ask_in[target_group[s], target_slot[s]]
        questions += [queries[0:16, :], queries[16:32, :]]
    mixed, stats = attention(questions, 16)
    for k in range(UNITS):
        for j in range(4):
            at = ((k % 2) * 4 + j) * 16 + (k // 2) * 4
            mixed_rows[at : at + 4, :] = mixed[k][j * 4 : j * 4 + 4, :]
            stats_rows[at : at + 4, :] = stats[k][j * 4 : j * 4 + 4, :]
    for k in range(N_CTX):
        part_out[k] = jnp.concatenate(
            [mixed_rows[k * 16 : k * 16 + 16, :], stats_rows[k * 16 : k * 16 + 16, :]], axis=0
        ).astype(BF16)
    part_in[c] = part_out[c]
    over_ctx(lambda p: send(part_out.at[p], part_in.at[c], PART, {"ctx": p}))
    for s in range(SLOTS):
        queries = ask_in[target_group[s], target_slot[s]].astype(F32)
        for k in range(N_CTX):
            asked[s * N_CTX + k] = queries[k * 4 : k * 4 + 4, :]

    arrived(new_in, NEW, N_DP - 1)
    for s in range(SLOTS):
        moved[s * 16 : s * 16 + 16, :] = new_in[target_group[s]].astype(F32)

    def lined_up(ref, row, stride):
        return jnp.concatenate([ref[pl.ds(row + ch, SLOTS, stride=stride), :] for ch in range(CHUNKS)], axis=1)

    for t in (1, 2):
        window = window[1:] + [lined_up(moved, (t - 1) * 4, 16)]
        filt[t, 0:SLOTS, :] = filtered(window)
    own = lax.broadcasted_iota(jnp.int32, (8, 128), 1) // 32 == lax.broadcasted_iota(jnp.int32, (8, 128), 0)
    picks = []
    for t in range(3):
        product = lax.dot_general(
            filt[t].astype(BF16), weight, (((1,), (1,)), ((), ())), preferred_element_type=F32
        )
        picks.append(jnp.sum(jnp.where(own, product, 0.0), axis=0, keepdims=True))
    arrived(one_part_in, ONE, N_CTX - 1)
    sel_out[0] = jnp.concatenate(picks + [jnp.zeros((1, 128), F32)], axis=0)
    sel_in[me] = sel_out[0]
    over_sel(lambda device: send(sel_out.at[0], sel_in.at[me], SELECT, device))

    def finish(part_in, rows, score, value):
        parts = [part_in[k].astype(F32) for k in range(N_CTX)]
        tops = [part[rows : 2 * rows, 0:1] for part in parts]
        overall = score
        for k in range(N_CTX):
            overall = jnp.maximum(overall, tops[k])
        denominator = jnp.exp(score - overall)
        numerator = value * denominator
        for k in range(N_CTX):
            keep = jnp.exp(tops[k] - overall)
            numerator += parts[k][0:rows, :] * keep
            denominator += (parts[k][rows : 2 * rows, 1:2] + parts[k][rows : 2 * rows, 2:3]) * keep
        return numerator / denominator, overall, denominator

    own_pair = fresh_one[c]
    one_out[0] = finish(one_part_in, 8, score_of(asked_one[c], own_pair[0:1, :]), own_pair[1:2, :])[0]
    one_in[c] = one_out[0]
    over_ctx(lambda p: send(one_out.at[0], one_in.at[c], ONE_DONE, {"ctx": p}))

    rates = jnp.exp(decay_ref[...])
    inputs = [filt[t, 0:SLOTS, :] for t in range(3)]
    for t in range(3):
        sizes = steps_ref[0] if t == 0 else lined_up(moved, 8 + (t - 1) * 4, 16)
        pushed[t, 0:SLOTS, :] = sizes * inputs[t]
        for s in range(SLOTS):
            decays[t, s] = jnp.exp(-sizes[s : s + 1, :] * rates)

    def leaves(s, p):
        return jnp.where(target_group[s] == p, 1.0, 0.0).astype(F32)

    def returned(rows, p):
        total = rows[0:8, :] * leaves(0, p)
        for s in range(1, SLOTS):
            total += rows[s * 8 : (s + 1) * 8, :] * leaves(s, p)
        return total

    first_score = score_of(head_rows(asked), pair_rows(fresh_one, 0))
    first_value = pair_rows(fresh_one, 1)
    arrived(part_in, PART, N_CTX - 1)
    done, overall, denominator = finish(part_in, 16, first_score, first_value)
    weight_log = jnp.broadcast_to(overall + jnp.log(denominator), (16, 128))
    for s in range(SLOTS):
        back_rows[s * 8 : s * 8 + 4, :] = done[s * 4 : s * 4 + 4, :]
        back_rows[s * 8 + 4 : s * 8 + 8, :] = weight_log[s * 4 : s * 4 + 4, :]

    def ans_one(p):
        ans_out[p] = returned(back_rows, p)
        send(ans_out.at[p], ans_in.at[d], ANSWER, {"dp": p})

    first_started(d, N_DP, ans_one)
    ans_in[d] = returned(back_rows, d)

    def gated(result, t):
        gate = inputs_ref[t, 1].astype(F32)
        return (result * (gate * jax.nn.sigmoid(gate))).astype(BF16)

    arrived(sel_in, SELECT, N_SEL - 1)
    total = sel_in[0]
    for k in range(1, N_SEL):
        total += sel_in[k]
    columns = jnp.transpose(jnp.concatenate([total, jnp.zeros((4, 128), F32)], axis=0))
    for s in range(SLOTS):
        hidden = state_ref[s]
        for t in range(3):
            into = columns[s * 32 : s * 32 + 16, t : t + 1]
            out = columns[s * 32 + 16 : s * 32 + 32, t : t + 1]
            hidden = decays[t, s] * hidden + into * pushed[t, s : s + 1, :]
            scan_rows[t, s : s + 1, :] = jnp.sum(out * hidden, axis=0, keepdims=True)
    for t in range(3):
        result = scan_rows[t, 0:SLOTS, :] + skip_ref[...] * inputs[t]
        if t == 0:
            mam_ref[0] = gated(result, 0)
        else:
            for ch in range(CHUNKS):
                mam_rows[pl.ds((t - 1) * 4 + ch, SLOTS, stride=8), :] = result[:, ch * 128 : (ch + 1) * 128]

    def mam_one(p):
        mam_out[p] = returned(mam_rows, p)
        send(mam_out.at[p], mam_in.at[d], MAMBA, {"dp": p})

    over_dp(mam_one)
    mam_in[d] = returned(mam_rows, d)

    def picked(ref, i):
        total = ref[0] * member[i, 0:1, :]
        for g in range(1, N_DP):
            total += ref[g] * member[i, g : g + 1, :]
        return total

    arrived(ans_in, ANSWER, N_DP - 1)
    found = [picked(ans_in, i) for i in range(SLOTS)]
    cached = jnp.concatenate([x[0:4, :] for x in found], axis=0)
    cached_log = jnp.concatenate([x[4:8, :] for x in found], axis=0)[:, 0:1]
    overall = jnp.maximum(cached_log, jnp.maximum(second_score, third_score))
    keeps = [jnp.exp(cached_log - overall), jnp.exp(second_score - overall)]
    keeps.append(jnp.where(last_step, jnp.exp(third_score - overall), 0.0))
    done = (cached * keeps[0] + second_value * keeps[1] + third_value * keeps[2]) / (keeps[0] + keeps[1] + keeps[2])
    fin_out[0] = done.astype(BF16)
    fin_in[c] = done.astype(BF16)
    over_ctx(lambda p: send(fin_out.at[0], fin_in.at[c], DONE, {"ctx": p}))

    arrived(one_in, ONE_DONE, N_CTX - 1)
    for s in range(SLOTS):
        for h in range(2):
            rows_old[s * 24 + h * 8 : s * 24 + h * 8 + 8, :] = one_in[s * 2 + h]
    for j in range(16):
        att_ref[0, :, j * 128 : (j + 1) * 128] = rows_old[pl.ds(j, SLOTS, stride=24), :].astype(BF16)

    arrived(mam_in, MAMBA, N_DP - 1)
    for i in range(SLOTS):
        mam_rows[i * 8 : (i + 1) * 8, :] = picked(mam_in, i)
    for t in (1, 2):
        mam_ref[t] = gated(lined_up(mam_rows, (t - 1) * 4, 8), t)

    sent(table_in, TABLE, N_DP - 1)
    sent(ask_in, ASK, N_DP // 2 - 1)
    sent(ask_in, FORWARD, N_DP // 2)
    sent(new_out, NEW, N_DP - 1)
    sent(one_part_out, ONE, N_CTX - 1)
    sent(sel_in, SELECT, N_SEL - 1)
    sent(part_out, PART, N_CTX - 1)
    sent(ans_out, ANSWER, N_DP - 1)
    sent(one_in, ONE_DONE, N_CTX - 1)
    sent(mam_out, MAMBA, N_DP - 1)

    arrived(fin_in, DONE, N_CTX - 1)
    for k in range(N_CTX):
        all_rows[k * 16 : (k + 1) * 16, :] = fin_in[k].astype(F32)
    for t in (1, 2):
        for j in range(16):
            att_ref[t, :, j * 128 : (j + 1) * 128] = all_rows[
                pl.ds((j // 2) * 16 + (j % 2) * 2 + t - 1, SLOTS, stride=4), :
            ].astype(BF16)
    sent(fin_in, DONE, N_CTX - 1)


def on_device(
    key_cache,
    value_cache,
    lengths,
    queries,
    fresh_pairs,
    recent_inputs,
    scan_state,
    mamba_inputs,
    step_sizes,
    filter_taps,
    filter_bias,
    decay_logs,
    skip_gain,
    select_weight,
    target_group,
    target_slot,
):
    vmem = pl.BlockSpec(memory_space=pltpu.VMEM)
    operands = (
        lengths,
        target_group,
        target_slot,
        key_cache,
        value_cache,
        queries,
        fresh_pairs,
        jnp.swapaxes(recent_inputs, 0, 1),
        scan_state,
        mamba_inputs,
        step_sizes,
        filter_taps,
        filter_bias.reshape(1, CHAN),
        decay_logs,
        skip_gain.reshape(1, CHAN),
        select_weight,
    )
    operands = tuple(pltpu.with_memory_space_constraint(x, pltpu.HBM) for x in operands)
    return pl.pallas_call(
        kernel,
        out_shape=(
            jax.ShapeDtypeStruct((3, SLOTS, 2048), BF16),
            jax.ShapeDtypeStruct((3, SLOTS, CHAN), BF16),
        ),
        in_specs=[pl.BlockSpec(memory_space=pltpu.HBM)] * 16,
        out_specs=(vmem, vmem),
        scratch_shapes=[pltpu.SMEM((SLOTS,), jnp.int32)] * 3
        + [pltpu.VMEM(x.shape, x.dtype) for x in operands[3:]]
        + [
            pltpu.SemaphoreType.DMA((16,)),
            pltpu.VMEM((1, 1, 128), jnp.int32),
            pltpu.VMEM((N_DP, 1, 128), jnp.int32),
            pltpu.VMEM((SLOTS, N_DP, 128), F32),
            pltpu.VMEM((SLOTS * 32, 128), F32),
            pltpu.VMEM((SLOTS * ROWS, 128), F32),
            pltpu.VMEM((SLOTS * 24, 128), F32),
            pltpu.VMEM((SLOTS, 32, 128), BF16),
            pltpu.VMEM((N_DP, SLOTS, 32, 128), BF16),
            pltpu.VMEM((N_DP, 16, 128), BF16),
            pltpu.VMEM((N_DP, 16, 128), BF16),
            pltpu.VMEM((SLOTS * 16, 128), F32),
            pltpu.VMEM((UNITS, 8, 128), F32),
            pltpu.VMEM((SLOTS * N_CTX, 4, 128), F32),
            pltpu.VMEM((SLOTS * N_CTX, 4, 128), F32),
            pltpu.VMEM((UNITS, 8, 128), F32),
            pltpu.VMEM((UNITS, 8, 128), F32),
            pltpu.VMEM((N_CTX * 16, 128), F32),
            pltpu.VMEM((N_CTX * 16, 128), F32),
            pltpu.VMEM((3, 8, CHAN), F32),
            pltpu.VMEM((1, 4, 128), F32),
            pltpu.VMEM((N_SEL, 4, 128), F32),
            pltpu.VMEM((N_CTX, 16, 128), BF16),
            pltpu.VMEM((N_CTX, 16, 128), BF16),
            pltpu.VMEM((N_CTX, 32, 128), BF16),
            pltpu.VMEM((N_CTX, 32, 128), BF16),
            pltpu.VMEM((1, 16, 128), BF16),
            pltpu.VMEM((N_CTX, 16, 128), BF16),
            pltpu.VMEM((1, 8, 128), F32),
            pltpu.VMEM((N_CTX, 8, 128), F32),
            pltpu.VMEM((3, SLOTS, 16, CHAN), F32),
            pltpu.VMEM((3, 8, CHAN), F32),
            pltpu.VMEM((3, 8, CHAN), F32),
            pltpu.VMEM((SLOTS * 8, 128), F32),
            pltpu.VMEM((N_DP, 8, 128), F32),
            pltpu.VMEM((N_DP, 8, 128), F32),
            pltpu.VMEM((N_DP, 8, 128), F32),
            pltpu.VMEM((N_DP, 8, 128), F32),
            pltpu.VMEM((SLOTS * 8, 128), F32),
            pltpu.VMEM((N_CTX * 16, 128), F32),
            pltpu.SemaphoreType.DMA((11,)),
            pltpu.SemaphoreType.DMA((11,)),
            pltpu.SemaphoreType.DMA((N_DP // 2,)),
        ],
        compiler_params=pltpu.CompilerParams(
            collective_id=0, has_side_effects=True, vmem_limit_bytes=32 * 2**20
        ),
    )(*operands)


def solution(mesh):
    placed = (
        P("dp", "ctx", "mp"),
        P("dp", "ctx", "mp"),
        P("dp"),
        P(None, "dp", "mp"),
        P(None, None, "dp", "mp"),
        P("dp", None, ("ctx", "mp")),
        P("dp", None, ("ctx", "mp")),
        P(None, None, "dp", ("ctx", "mp")),
        P(None, "dp", ("ctx", "mp")),
        P(None, ("ctx", "mp")),
        P(("ctx", "mp")),
        P(None, ("ctx", "mp")),
        P(("ctx", "mp")),
        P(None, ("ctx", "mp")),
        P("dp"),
        P("dp"),
    )
    return jax.shard_map(
        on_device,
        mesh=mesh,
        in_specs=placed,
        out_specs=(P(None, "dp", "mp"), P(None, "dp", ("ctx", "mp"))),
        check_vma=False,
    )
```

```python
import functools

import jax
import jax.numpy as jnp
from jax import lax
from jax.experimental import pallas as pl
from jax.experimental.pallas import tpu as pltpu
from jax.sharding import PartitionSpec as P

HEAD = 128
NEGATIVE = -1e30
SCALE = HEAD**-0.5
MESH = pl.DeviceIdType.MESH
F32 = jnp.float32
BF16 = jnp.bfloat16

N_DP = 16
N_CTX = 8
N_MP = 4
N_SEL = N_CTX * N_MP
SLOTS = 4
UNITS = 8
BLOCK = 256
CHAN = 512
CHUNKS = CHAN // 128

ROW_M = 0
ROW_S = 8
ROWS = 16

FIRST_LOADS = (1, 2, 5)
LATER_LOADS = (6, 9, 10, 0, 3, 4, 7, 11, 12, 15, 8, 13, 14)

TABLE, ASK, ONE, NEW, PART, SELECT, ONE_DONE, DONE, MAMBA, ANSWER, FORWARD = range(11)


def kernel(*refs):
    operands, (att_ref, mam_ref), rest = refs[:16], refs[16:18], refs[18:]
    local, in_sem, rest = rest[:16], rest[16], rest[17:]
    run(operands, local, in_sem, att_ref, mam_ref, *rest)


def run(
    operands,
    local,
    in_sem,
    att_ref,
    mam_ref,
    table_out,
    table_in,
    member,
    rows_ask,
    rows_new,
    rows_old,
    ask_out,
    ask_in,
    new_out,
    new_in,
    moved,
    asked_one,
    asked,
    asked_new,
    fresh_one,
    fresh_new,
    mixed_rows,
    stats_rows,
    filt,
    sel_out,
    sel_in,
    one_part_out,
    one_part_in,
    part_out,
    part_in,
    fin_out,
    fin_in,
    one_out,
    one_in,
    decays,
    pushed,
    scan_rows,
    mam_rows,
    mam_out,
    mam_in,
    ans_out,
    ans_in,
    back_rows,
    all_rows,
    send_sem,
    recv_sem,
    ask_sem,
):
    (lengths, target_group, target_slot, key_ref, value_ref, query_ref, fresh_ref, recent_ref) = local[:8]
    (state_ref, inputs_ref, steps_ref, taps_ref, bias_ref, decay_ref, skip_ref, select_ref) = local[8:]
    loads = [pltpu.make_async_copy(operands[k], local[k], in_sem.at[k]) for k in range(16)]
    for k in FIRST_LOADS:
        loads[k].start()

    d = lax.axis_index("dp")
    c = lax.axis_index("ctx")
    m = lax.axis_index("mp")
    me = c * N_MP + m
    partner = d + 1 - 2 * (d % 2)

    def far_first(here, count, fn):
        def body(k, carry):
            step = (k + 1) // 2
            p = here + count // 2 + jnp.where(k == 2 * step, step, -step)
            fn(jnp.where(p >= count, p - count, p))
            return carry

        lax.fori_loop(0, count - 1, body, 0)

    def first_started(here, count, fn):
        def body(k, carry):
            fn(k + jnp.where(k >= here, 1, 0))
            return carry

        lax.fori_loop(0, count - 1, body, 0)

    def over_dp(fn):
        far_first(d, N_DP, fn)

    def over_ctx(fn):
        far_first(c, N_CTX, fn)

    def over_mp(fn):
        far_first(m, N_MP, fn)

    def over_sel(fn):
        far_first(me, N_SEL, lambda p: fn({"ctx": p // N_MP, "mp": p % N_MP}))

    def send(src, dst, phase, device):
        pltpu.make_async_remote_copy(
            src_ref=src,
            dst_ref=dst,
            send_sem=send_sem.at[phase],
            recv_sem=recv_sem.at[phase],
            device_id=device,
            device_id_type=MESH,
        ).start()

    def arrived(buffer, phase, count):
        part = buffer.at[pl.ds(0, count)]
        pltpu.make_async_copy(part, part, recv_sem.at[phase]).wait()

    def sent(buffer, phase, count):
        part = buffer.at[pl.ds(0, count)]
        pltpu.make_async_copy(part, part, send_sem.at[phase]).wait()

    barrier = pltpu.get_barrier_semaphore()

    def greet(device):
        pl.semaphore_signal(barrier, inc=1, device_id=device, device_id_type=MESH)

    over_dp(lambda p: greet({"dp": p}))
    over_ctx(lambda p: greet({"ctx": p}))
    over_mp(lambda p: greet({"mp": p}))
    for k in LATER_LOADS:
        loads[k].start()

    loads[1].wait()
    loads[2].wait()
    lane = lax.broadcasted_iota(jnp.int32, (1, 128), 1)
    landing = jnp.full((1, 128), -1, jnp.int32)
    for s in range(SLOTS):
        landing = jnp.where(lane == s, target_group[s] * SLOTS + target_slot[s], landing)
    table_out[0] = landing
    table_in[d] = landing
    loads[5].wait()
    for t in (1, 2):
        q = query_ref[t].astype(F32)
        for j in range(16):
            rows_ask[pl.ds(j * 2 + t - 1, SLOTS, stride=32), :] = q[:, j * 128 : (j + 1) * 128]
    for s in range(SLOTS):
        ask_out[s] = rows_ask[s * 32 : s * 32 + 32, :].astype(BF16)
        ask_in[d, s] = ask_out[s]
    pl.semaphore_wait(barrier, (N_DP - 1) + (N_CTX - 1) + (N_MP - 1))

    over_dp(lambda p: send(table_out.at[0], table_in.at[d], TABLE, {"dp": p}))

    def ask_one(k, carry):
        step = (k + 1) // 2
        p = d + N_DP // 2 + 2 * jnp.where(k == 2 * step, step, -step)
        pltpu.make_async_remote_copy(
            src_ref=ask_out,
            dst_ref=ask_in.at[d],
            send_sem=send_sem.at[ASK],
            recv_sem=ask_sem.at[d // 2],
            device_id={"dp": jnp.where(p >= N_DP, p - N_DP, p)},
            device_id_type=MESH,
        ).start()
        return carry

    lax.fori_loop(0, N_DP // 2 - 1, ask_one, 0)
    send(ask_out, ask_in.at[d], FORWARD, {"dp": partner})

    for k in (6, 9, 10):
        loads[k].wait()
    for t in (1, 2):
        x = inputs_ref[t, 0].astype(F32)
        for ch in range(CHUNKS):
            rows_new[pl.ds(ROW_M + (t - 1) * 4 + ch, SLOTS, stride=ROWS), :] = x[:, ch * 128 : (ch + 1) * 128]
        x = steps_ref[t]
        for ch in range(CHUNKS):
            rows_new[pl.ds(ROW_S + (t - 1) * 4 + ch, SLOTS, stride=ROWS), :] = x[:, ch * 128 : (ch + 1) * 128]
    q = query_ref[0].astype(F32)
    for j in range(16):
        rows_old[pl.ds(j, SLOTS, stride=24), :] = q[:, j * 128 : (j + 1) * 128]
    for kv in range(2):
        f = fresh_ref[0, kv].astype(F32)
        for h in range(2):
            rows_old[pl.ds(16 + kv * 2 + h, SLOTS, stride=24), :] = f[:, h * 128 : (h + 1) * 128]

    units = [(s, h) for s in range(SLOTS) for h in range(2)]

    def attention(questions, rows):
        positions = lax.broadcasted_iota(jnp.int32, (rows, BLOCK), 1) + c * BLOCK
        lanes = lax.broadcasted_iota(jnp.int32, (rows, 128), 1)
        scores = [
            lax.dot_general(
                questions[k],
                key_ref[s, :, h * 128 : (h + 1) * 128],
                (((1,), (1,)), ((), ())),
                preferred_element_type=F32,
            )
            * SCALE
            for k, (s, h) in enumerate(units)
        ]
        usable = [positions < lengths[s] for s, h in units]
        scores = [jnp.where(usable[k], scores[k], NEGATIVE) for k in range(UNITS)]
        tops = [jnp.max(x, axis=1, keepdims=True).astype(BF16).astype(F32) for x in scores]
        weights = [jnp.where(usable[k], jnp.exp(scores[k] - tops[k]), 0.0) for k in range(UNITS)]
        totals = [jnp.sum(x, axis=1, keepdims=True) for x in weights]
        mixed = [
            jnp.dot(weights[k].astype(BF16), value_ref[s, :, h * 128 : (h + 1) * 128], preferred_element_type=F32)
            for k, (s, h) in enumerate(units)
        ]
        stats = []
        for k in range(UNITS):
            high = totals[k].astype(BF16).astype(F32)
            stats.append(jnp.where(lanes == 0, tops[k], jnp.where(lanes == 1, high, totals[k] - high)))
        return mixed, stats

    for s in range(SLOTS):
        for h in range(2):
            asked_one[s * 2 + h] = rows_old[s * 24 + h * 8 : s * 24 + h * 8 + 8, :]
            fresh_one[s * 2 + h] = jnp.concatenate(
                [
                    rows_old[s * 24 + 16 + h : s * 24 + 17 + h, :],
                    rows_old[s * 24 + 18 + h : s * 24 + 19 + h, :],
                    jnp.zeros((6, 128), F32),
                ],
                axis=0,
            )
    for k in (0, 3, 4):
        loads[k].wait()
    mixed, stats = attention([asked_one[k].astype(BF16) for k in range(UNITS)], 8)
    for k in range(UNITS):
        one_part_out[k] = jnp.concatenate([mixed[k], stats[k]], axis=0).astype(BF16)
    one_part_in[c] = one_part_out[c]
    over_ctx(lambda p: send(one_part_out.at[p], one_part_in.at[c], ONE, {"ctx": p}))

    arrived(table_in, TABLE, N_DP - 1)
    table = table_in[...].reshape(N_DP, 128)
    for i in range(SLOTS):
        hit = jnp.where(table == d * SLOTS + i, 1.0, 0.0).astype(F32)
        member[i] = jnp.broadcast_to(jnp.max(hit, axis=1, keepdims=True), (N_DP, 128))

    def chosen(p, first, last):
        total = rows_new[first:last, :] * member[0, pl.ds(p, 1), :]
        for i in range(1, SLOTS):
            total += rows_new[i * ROWS + first : i * ROWS + last, :] * member[i, pl.ds(p, 1), :]
        return total

    def message(first, last, out, into, phase):
        def one(p):
            out[p] = chosen(p, first, last).astype(out.dtype)
            send(out.at[p], into.at[d], phase, {"dp": p})

        over_dp(one)
        into[d] = chosen(d, first, last).astype(out.dtype)

    message(ROW_M, ROWS, new_out, new_in, NEW)

    def forward(k, carry):
        step = k // 2 + 1
        p = d + 2 * jnp.where(k == 2 * step - 2, step, N_DP // 2 - step)
        group = jnp.where(p >= N_DP, p - N_DP, p)
        block = ask_in.at[group]
        pltpu.make_async_copy(block, block, ask_sem.at[group // 2]).wait()
        send(block, block, FORWARD, {"dp": partner})
        return carry

    lax.fori_loop(0, N_DP // 2 - 1, forward, 0)

    for s in range(SLOTS):
        for k in range(N_CTX):
            asked_new[s * N_CTX + k] = rows_ask[s * 32 + k * 4 : s * 32 + k * 4 + 4, :]
    for t in (1, 2):
        for kv in range(2):
            f = fresh_ref[t, kv].astype(F32)
            for s in range(SLOTS):
                for h in range(2):
                    fresh_new[s * 2 + h, (t - 1) * 2 + kv : (t - 1) * 2 + kv + 1, :] = f[s : s + 1, h * 128 : (h + 1) * 128]
    kv_head = c // (N_CTX // 2)

    def pair_rows(ref, row):
        return jnp.concatenate(
            [jnp.broadcast_to(ref[s * 2 + kv_head, row : row + 1, :], (4, 128)) for s in range(SLOTS)], axis=0
        )

    def head_rows(ref):
        return jnp.concatenate([ref[s * N_CTX + c] for s in range(SLOTS)], axis=0)

    def score_of(questions, keys):
        return jnp.sum(questions * keys, axis=1, keepdims=True) * SCALE

    own_asks = head_rows(asked_new)
    last_step = lax.broadcasted_iota(jnp.int32, (16, 1), 0) % 2 == 1
    second_score = score_of(own_asks, pair_rows(fresh_new, 0))
    third_score = jnp.where(last_step, score_of(own_asks, pair_rows(fresh_new, 2)), NEGATIVE)
    second_value = pair_rows(fresh_new, 1)
    third_value = pair_rows(fresh_new, 3)

    for k in (7, 8, 11, 12, 13, 14, 15):
        loads[k].wait()
    taps = taps_ref[...].astype(F32)
    bias = bias_ref[...]
    window = [recent_ref[k].astype(F32) for k in range(3)] + [inputs_ref[0, 0].astype(F32)]

    def filtered(parts):
        total = parts[0] * taps[0:1, :]
        for k in range(1, 4):
            total += parts[k] * taps[k : k + 1, :]
        total += bias
        return (total * jax.nn.sigmoid(total)).astype(BF16).astype(F32)

    filt[0, 0:SLOTS, :] = filtered(window)
    weight = select_ref[...]
    weight = jnp.concatenate([weight] * SLOTS, axis=0)

    arrived(ask_in, FORWARD, N_DP // 2)
    questions = []
    for s in range(SLOTS):
        queries = ask_in[target_group[s], target_slot[s]]
        questions += [queries[0:16, :], queries[16:32, :]]
    mixed, stats = attention(questions, 16)
    for k in range(UNITS):
        for j in range(4):
            at = ((k % 2) * 4 + j) * 16 + (k // 2) * 4
            mixed_rows[at : at + 4, :] = mixed[k][j * 4 : j * 4 + 4, :]
            stats_rows[at : at + 4, :] = stats[k][j * 4 : j * 4 + 4, :]
    for k in range(N_CTX):
        part_out[k] = jnp.concatenate(
            [mixed_rows[k * 16 : k * 16 + 16, :], stats_rows[k * 16 : k * 16 + 16, :]], axis=0
        ).astype(BF16)
    part_in[c] = part_out[c]
    over_ctx(lambda p: send(part_out.at[p], part_in.at[c], PART, {"ctx": p}))
    for s in range(SLOTS):
        queries = ask_in[target_group[s], target_slot[s]].astype(F32)
        for k in range(N_CTX):
            asked[s * N_CTX + k] = queries[k * 4 : k * 4 + 4, :]

    arrived(new_in, NEW, N_DP - 1)
    for s in range(SLOTS):
        moved[s * 16 : s * 16 + 16, :] = new_in[target_group[s]].astype(F32)

    def lined_up(ref, row, stride):
        return jnp.concatenate([ref[pl.ds(row + ch, SLOTS, stride=stride), :] for ch in range(CHUNKS)], axis=1)

    for t in (1, 2):
        window = window[1:] + [lined_up(moved, (t - 1) * 4, 16)]
        filt[t, 0:SLOTS, :] = filtered(window)
    own = lax.broadcasted_iota(jnp.int32, (8, 128), 1) // 32 == lax.broadcasted_iota(jnp.int32, (8, 128), 0)
    picks = []
    for t in range(3):
        product = lax.dot_general(
            filt[t].astype(BF16), weight, (((1,), (1,)), ((), ())), preferred_element_type=F32
        )
        picks.append(jnp.sum(jnp.where(own, product, 0.0), axis=0, keepdims=True))
    arrived(one_part_in, ONE, N_CTX - 1)
    sel_out[0] = jnp.concatenate(picks + [jnp.zeros((1, 128), F32)], axis=0)
    sel_in[me] = sel_out[0]
    over_sel(lambda device: send(sel_out.at[0], sel_in.at[me], SELECT, device))

    def finish(part_in, rows, score, value):
        parts = [part_in[k].astype(F32) for k in range(N_CTX)]
        tops = [part[rows : 2 * rows, 0:1] for part in parts]
        overall = score
        for k in range(N_CTX):
            overall = jnp.maximum(overall, tops[k])
        denominator = jnp.exp(score - overall)
        numerator = value * denominator
        for k in range(N_CTX):
            keep = jnp.exp(tops[k] - overall)
            numerator += parts[k][0:rows, :] * keep
            denominator += (parts[k][rows : 2 * rows, 1:2] + parts[k][rows : 2 * rows, 2:3]) * keep
        return numerator / denominator, overall, denominator

    own_pair = fresh_one[c]
    one_out[0] = finish(one_part_in, 8, score_of(asked_one[c], own_pair[0:1, :]), own_pair[1:2, :])[0]
    one_in[c] = one_out[0]
    over_ctx(lambda p: send(one_out.at[0], one_in.at[c], ONE_DONE, {"ctx": p}))

    rates = jnp.exp(decay_ref[...])
    inputs = [filt[t, 0:SLOTS, :] for t in range(3)]
    for t in range(3):
        sizes = steps_ref[0] if t == 0 else lined_up(moved, 8 + (t - 1) * 4, 16)
        pushed[t, 0:SLOTS, :] = sizes * inputs[t]
        for s in range(SLOTS):
            decays[t, s] = jnp.exp(-sizes[s : s + 1, :] * rates)

    def leaves(s, p):
        return jnp.where(target_group[s] == p, 1.0, 0.0).astype(F32)

    def returned(rows, p):
        total = rows[0:8, :] * leaves(0, p)
        for s in range(1, SLOTS):
            total += rows[s * 8 : (s + 1) * 8, :] * leaves(s, p)
        return total

    first_score = score_of(head_rows(asked), pair_rows(fresh_one, 0))
    first_value = pair_rows(fresh_one, 1)
    arrived(part_in, PART, N_CTX - 1)
    done, overall, denominator = finish(part_in, 16, first_score, first_value)
    place = lax.broadcasted_iota(jnp.int32, (16, 128), 1) == lax.broadcasted_iota(jnp.int32, (16, 128), 0) % 4
    weight_log = jnp.where(place, overall + jnp.log(denominator), 0.0)
    for s in range(SLOTS):
        back_rows[s * 8 : s * 8 + 4, :] = done[s * 4 : s * 4 + 4, :]
        logs = jnp.sum(weight_log[s * 4 : s * 4 + 4, :], axis=0, keepdims=True)
        back_rows[s * 8 + 4 : s * 8 + 8, :] = jnp.broadcast_to(logs, (4, 128))

    def ans_one(p):
        ans_out[p] = returned(back_rows, p)
        send(ans_out.at[p, pl.ds(0, 5)], ans_in.at[d, pl.ds(0, 5)], ANSWER, {"dp": p})

    first_started(d, N_DP, ans_one)
    ans_in[d] = returned(back_rows, d)

    def gated(result, t):
        gate = inputs_ref[t, 1].astype(F32)
        return (result * (gate * jax.nn.sigmoid(gate))).astype(BF16)

    arrived(sel_in, SELECT, N_SEL - 1)
    total = sel_in[0]
    for k in range(1, N_SEL):
        total += sel_in[k]
    columns = jnp.transpose(jnp.concatenate([total, jnp.zeros((4, 128), F32)], axis=0))
    for s in range(SLOTS):
        hidden = state_ref[s]
        for t in range(3):
            into = columns[s * 32 : s * 32 + 16, t : t + 1]
            out = columns[s * 32 + 16 : s * 32 + 32, t : t + 1]
            hidden = decays[t, s] * hidden + into * pushed[t, s : s + 1, :]
            scan_rows[t, s : s + 1, :] = jnp.sum(out * hidden, axis=0, keepdims=True)
    for t in range(3):
        result = scan_rows[t, 0:SLOTS, :] + skip_ref[...] * inputs[t]
        if t == 0:
            mam_ref[0] = gated(result, 0)
        else:
            for ch in range(CHUNKS):
                mam_rows[pl.ds((t - 1) * 4 + ch, SLOTS, stride=8), :] = result[:, ch * 128 : (ch + 1) * 128]

    def mam_one(p):
        mam_out[p] = returned(mam_rows, p)
        send(mam_out.at[p], mam_in.at[d], MAMBA, {"dp": p})

    over_dp(mam_one)
    mam_in[d] = returned(mam_rows, d)

    def picked(ref, i, rows=8):
        total = ref[0, 0:rows, :] * member[i, 0:1, :]
        for g in range(1, N_DP):
            total += ref[g, 0:rows, :] * member[i, g : g + 1, :]
        return total

    arrived(ans_in.at[:, pl.ds(0, 5)], ANSWER, N_DP - 1)
    found = [picked(ans_in, i, 5) for i in range(SLOTS)]
    cached = jnp.concatenate([x[0:4, :] for x in found], axis=0)
    logs = jnp.concatenate([jnp.broadcast_to(x[4:5, :], (4, 128)) for x in found], axis=0)
    cached_log = jnp.sum(jnp.where(place, logs, 0.0), axis=1, keepdims=True)
    overall = jnp.maximum(cached_log, jnp.maximum(second_score, third_score))
    keeps = [jnp.exp(cached_log - overall), jnp.exp(second_score - overall)]
    keeps.append(jnp.where(last_step, jnp.exp(third_score - overall), 0.0))
    done = (cached * keeps[0] + second_value * keeps[1] + third_value * keeps[2]) / (keeps[0] + keeps[1] + keeps[2])
    fin_out[0] = done.astype(BF16)
    fin_in[c] = done.astype(BF16)
    over_ctx(lambda p: send(fin_out.at[0], fin_in.at[c], DONE, {"ctx": p}))

    arrived(one_in, ONE_DONE, N_CTX - 1)
    for s in range(SLOTS):
        for h in range(2):
            rows_old[s * 24 + h * 8 : s * 24 + h * 8 + 8, :] = one_in[s * 2 + h]
    for j in range(16):
        att_ref[0, :, j * 128 : (j + 1) * 128] = rows_old[pl.ds(j, SLOTS, stride=24), :].astype(BF16)

    arrived(mam_in, MAMBA, N_DP - 1)
    for i in range(SLOTS):
        mam_rows[i * 8 : (i + 1) * 8, :] = picked(mam_in, i)
    for t in (1, 2):
        mam_ref[t] = gated(lined_up(mam_rows, (t - 1) * 4, 8), t)

    sent(table_in, TABLE, N_DP - 1)
    sent(ask_in, ASK, N_DP // 2 - 1)
    sent(ask_in, FORWARD, N_DP // 2)
    sent(new_out, NEW, N_DP - 1)
    sent(one_part_out, ONE, N_CTX - 1)
    sent(sel_in, SELECT, N_SEL - 1)
    sent(part_out, PART, N_CTX - 1)
    sent(ans_out.at[:, pl.ds(0, 5)], ANSWER, N_DP - 1)
    sent(one_in, ONE_DONE, N_CTX - 1)
    sent(mam_out, MAMBA, N_DP - 1)

    arrived(fin_in, DONE, N_CTX - 1)
    for k in range(N_CTX):
        all_rows[k * 16 : (k + 1) * 16, :] = fin_in[k].astype(F32)
    for t in (1, 2):
        for j in range(16):
            att_ref[t, :, j * 128 : (j + 1) * 128] = all_rows[
                pl.ds((j // 2) * 16 + (j % 2) * 2 + t - 1, SLOTS, stride=4), :
            ].astype(BF16)
    sent(fin_in, DONE, N_CTX - 1)


def on_device(
    key_cache,
    value_cache,
    lengths,
    queries,
    fresh_pairs,
    recent_inputs,
    scan_state,
    mamba_inputs,
    step_sizes,
    filter_taps,
    filter_bias,
    decay_logs,
    skip_gain,
    select_weight,
    target_group,
    target_slot,
):
    vmem = pl.BlockSpec(memory_space=pltpu.VMEM)
    operands = (
        lengths,
        target_group,
        target_slot,
        key_cache,
        value_cache,
        queries,
        fresh_pairs,
        jnp.swapaxes(recent_inputs, 0, 1),
        scan_state,
        mamba_inputs,
        step_sizes,
        filter_taps,
        filter_bias.reshape(1, CHAN),
        decay_logs,
        skip_gain.reshape(1, CHAN),
        select_weight,
    )
    operands = tuple(pltpu.with_memory_space_constraint(x, pltpu.HBM) for x in operands)
    return pl.pallas_call(
        kernel,
        out_shape=(
            jax.ShapeDtypeStruct((3, SLOTS, 2048), BF16),
            jax.ShapeDtypeStruct((3, SLOTS, CHAN), BF16),
        ),
        in_specs=[pl.BlockSpec(memory_space=pltpu.HBM)] * 16,
        out_specs=(vmem, vmem),
        scratch_shapes=[pltpu.SMEM((SLOTS,), jnp.int32)] * 3
        + [pltpu.VMEM(x.shape, x.dtype) for x in operands[3:]]
        + [
            pltpu.SemaphoreType.DMA((16,)),
            pltpu.VMEM((1, 1, 128), jnp.int32),
            pltpu.VMEM((N_DP, 1, 128), jnp.int32),
            pltpu.VMEM((SLOTS, N_DP, 128), F32),
            pltpu.VMEM((SLOTS * 32, 128), F32),
            pltpu.VMEM((SLOTS * ROWS, 128), F32),
            pltpu.VMEM((SLOTS * 24, 128), F32),
            pltpu.VMEM((SLOTS, 32, 128), BF16),
            pltpu.VMEM((N_DP, SLOTS, 32, 128), BF16),
            pltpu.VMEM((N_DP, 16, 128), BF16),
            pltpu.VMEM((N_DP, 16, 128), BF16),
            pltpu.VMEM((SLOTS * 16, 128), F32),
            pltpu.VMEM((UNITS, 8, 128), F32),
            pltpu.VMEM((SLOTS * N_CTX, 4, 128), F32),
            pltpu.VMEM((SLOTS * N_CTX, 4, 128), F32),
            pltpu.VMEM((UNITS, 8, 128), F32),
            pltpu.VMEM((UNITS, 8, 128), F32),
            pltpu.VMEM((N_CTX * 16, 128), F32),
            pltpu.VMEM((N_CTX * 16, 128), F32),
            pltpu.VMEM((3, 8, CHAN), F32),
            pltpu.VMEM((1, 4, 128), F32),
            pltpu.VMEM((N_SEL, 4, 128), F32),
            pltpu.VMEM((N_CTX, 16, 128), BF16),
            pltpu.VMEM((N_CTX, 16, 128), BF16),
            pltpu.VMEM((N_CTX, 32, 128), BF16),
            pltpu.VMEM((N_CTX, 32, 128), BF16),
            pltpu.VMEM((1, 16, 128), BF16),
            pltpu.VMEM((N_CTX, 16, 128), BF16),
            pltpu.VMEM((1, 8, 128), F32),
            pltpu.VMEM((N_CTX, 8, 128), F32),
            pltpu.VMEM((3, SLOTS, 16, CHAN), F32),
            pltpu.VMEM((3, 8, CHAN), F32),
            pltpu.VMEM((3, 8, CHAN), F32),
            pltpu.VMEM((SLOTS * 8, 128), F32),
            pltpu.VMEM((N_DP, 8, 128), F32),
            pltpu.VMEM((N_DP, 8, 128), F32),
            pltpu.VMEM((N_DP, 8, 128), F32),
            pltpu.VMEM((N_DP, 8, 128), F32),
            pltpu.VMEM((SLOTS * 8, 128), F32),
            pltpu.VMEM((N_CTX * 16, 128), F32),
            pltpu.SemaphoreType.DMA((11,)),
            pltpu.SemaphoreType.DMA((11,)),
            pltpu.SemaphoreType.DMA((N_DP // 2,)),
        ],
        compiler_params=pltpu.CompilerParams(
            collective_id=0, has_side_effects=True, vmem_limit_bytes=32 * 2**20
        ),
    )(*operands)


def solution(mesh):
    placed = (
        P("dp", "ctx", "mp"),
        P("dp", "ctx", "mp"),
        P("dp"),
        P(None, "dp", "mp"),
        P(None, None, "dp", "mp"),
        P("dp", None, ("ctx", "mp")),
        P("dp", None, ("ctx", "mp")),
        P(None, None, "dp", ("ctx", "mp")),
        P(None, "dp", ("ctx", "mp")),
        P(None, ("ctx", "mp")),
        P(("ctx", "mp")),
        P(None, ("ctx", "mp")),
        P(("ctx", "mp")),
        P(None, ("ctx", "mp")),
        P("dp"),
        P("dp"),
    )
    return jax.shard_map(
        on_device,
        mesh=mesh,
        in_specs=placed,
        out_specs=(P(None, "dp", "mp"), P(None, "dp", ("ctx", "mp"))),
        check_vma=False,
    )
```
